32 devices in a mesh: dp: 8 (over z, core), tensor: 4 (over y, x).
Axes of the slice: x: 2, y: 2, z: 4, core: 2. Of those that a mesh axis runs over, the one named last changes fastest.
Arguments:
- hidden: bfloat16 [1024, 18432], P('dp', 'tensor'), may hold values from -66 to 66
- grad_out: bfloat16 [1024, 4608], P('dp'), may hold values from -192 to 192
- seg_ids: int32 [1024], replicated, may hold values from 0 to 7, as said below
- seg_counts: int32 [64], P('dp'), may hold values from 1 to 31, as said below
- added_noise: bfloat16 [4608, 18432], P('dp', 'tensor'), may hold values from -6 to 6
Outputs:
- weight_grad: bfloat16 [4608, 18432], P('dp', 'tensor')
- example_norms: float32 [64], P('dp')
The draws below stay inside these ranges and needn't reach their ends.
Inputs may be any that keep to these rules, and one draw needn't show every extreme that they name: `seg_ids`: within each sequence the ids never fall and every one of the 8 ids occurs. seg_counts[j * 8 + i] is the number of tokens of sequence j whose id is i; the counts of a sequence sum to 128.
All inputs are finite; a program needn't handle non-finite values.
Results may differ from the reference program's by a relative error of at most 0.012.
Values may be sent and summed in bfloat16 or wider, within the bound.
A program may use at most 64 MiB of HBM per device.

```python
import math
import jax
import jax.numpy as jnp
from jax import lax

D = 4608
FFW = 18432
SEQ = 128
NSEG = 8
TOKENS = 1024
EXAMPLES = 64


def segment_lengths(key):
    groups = TOKENS // SEQ
    width = SEQ // NSEG
    key_shift, key_order = jax.random.split(key)
    shifts = jax.random.randint(key_shift, (groups, NSEG // 2), 1 - width, width)
    shifts = shifts.at[:, 0].set(width - 1)
    lengths = jnp.concatenate([width + shifts, width - shifts], axis=1)
    order_keys = jax.random.split(key_order, groups)
    permuted = jax.vmap(lambda item_key: jax.random.permutation(item_key, NSEG))(order_keys)
    return jnp.take_along_axis(lengths, permuted, axis=1).astype(jnp.int32)


def token_segments(lengths):
    bounds = jnp.cumsum(lengths, axis=1)
    positions = jnp.arange(SEQ, dtype=jnp.int32)
    return jnp.sum((positions[None, :, None] >= bounds[:, None, :NSEG - 1]).astype(jnp.int32), axis=2).astype(jnp.int32)


def draw_seg_counts(key, part):
    lengths = segment_lengths(key)
    return lengths.reshape(EXAMPLES).astype(jnp.int32)


def draw_seg_ids(key, part):
    segments = token_segments(segment_lengths(key))
    return segments.reshape(TOKENS).astype(jnp.int32)


def scaled_field(key, rows, columns, spread, entries):
    key_rows, key_columns = jax.random.split(key)
    reach = math.log(spread)
    row_scale = jnp.exp(jax.random.uniform(key_rows, (rows, 1), jnp.float32, -reach, reach))
    column_scale = jnp.exp(jax.random.uniform(key_columns, (1, columns), jnp.float32, -reach, reach))
    return entries * row_scale * column_scale


def draw_hidden(key, part):
    key = jax.random.fold_in(key, 5)
    key_main = jax.random.fold_in(key, 0)
    key_scale = jax.random.fold_in(key, 2)
    entries = jnp.clip(jax.random.normal(key_main, (TOKENS, FFW), jnp.float32), -6.0, 6.0)
    spread = 3.1622777
    return scaled_field(key_scale, TOKENS, FFW, spread, entries).astype(jnp.bfloat16)


def draw_grad_out(key, part):
    segments = token_segments(segment_lengths(key))
    key = jax.random.fold_in(key, 6)
    key_main = jax.random.fold_in(key, 0)
    key_scale = jax.random.fold_in(key, 2)
    key_example = jax.random.fold_in(key, 3)
    groups = TOKENS // SEQ
    example_scale = jnp.exp(jax.random.uniform(key_example, (groups, NSEG), jnp.float32, -1.0986123, 1.0986123))
    tok_scale = jnp.take_along_axis(example_scale, segments, axis=1).reshape(TOKENS, 1)
    entries = jnp.clip(jax.random.normal(key_main, (TOKENS, D), jnp.float32), -6.0, 6.0)
    spread = 3.1622777
    field = scaled_field(key_scale, TOKENS, D, spread, entries) * tok_scale
    return field.astype(jnp.bfloat16)


def levels(own_key, extent, shards, least, high):
    gain = 1.0
    for axis_at, shards_of in shards:
        draws = jax.random.uniform(jax.random.fold_in(jax.random.fold_in(own_key, 6), axis_at), (shards_of,), jnp.float32, least / len(shards), high / len(shards))
        gain = gain * jnp.repeat(jnp.exp(draws), extent[axis_at] // shards_of).reshape((-1,) + (1,) * (len(extent) - 1 - axis_at))
    return gain


def centred(stream_key, dims, scale, most, pieces=(), kind=jnp.bfloat16):
    factor_of = levels(stream_key, dims, pieces, -0.22, 0.18) if pieces else 1.0
    drawn = jax.random.normal(stream_key, dims, jnp.float32) * scale * factor_of
    return jnp.minimum(jnp.maximum(drawn, -most), most).astype(kind)


def setup_inputs(seed: int = 0) -> dict:
    splits = jax.random.split(jax.random.key(seed), 6)
    hidden = draw_hidden(jax.random.fold_in(splits[5], 71), 0)
    grad_out = draw_grad_out(jax.random.fold_in(splits[5], 71), 0)
    seg_ids = draw_seg_ids(jax.random.fold_in(splits[5], 71), 0)
    seg_counts = draw_seg_counts(jax.random.fold_in(splits[5], 71), 0)
    added_noise = centred(splits[4], (D, FFW), 1.0, 6.0, ((0, 8), (1, 4)))
    return {"hidden": hidden, "grad_out": grad_out, "seg_ids": seg_ids, "seg_counts": seg_counts, "added_noise": added_noise}


EPSILON = 1e-06
CLIP_FRACTION = 4.2

def clip_bound():
    return CLIP_FRACTION * (FFW * D * NSEG / SEQ) ** 0.5

def group_squares(item):
    hidden_group, scaled_group, segment_group = item
    hidden_wide = hidden_group.astype(jnp.float32)
    scaled_wide = scaled_group.astype(jnp.float32)
    gram_hidden = jnp.dot(hidden_wide, hidden_wide.T, precision=lax.Precision.HIGHEST)
    gram_scaled = jnp.dot(scaled_wide, scaled_wide.T, precision=lax.Precision.HIGHEST)
    member = (segment_group[:, None] == jnp.arange(NSEG, dtype=jnp.int32)[None, :]).astype(jnp.float32)
    products = gram_hidden * gram_scaled
    return lax.optimization_barrier(jnp.sum(member * jnp.dot(products, member, precision=lax.Precision.HIGHEST), axis=0))

def reference(hidden, grad_out, seg_ids, seg_counts, added_noise):
    groups = TOKENS // SEQ
    segments = seg_ids.reshape(groups, SEQ).astype(jnp.int32)
    counts = seg_counts.reshape(groups, NSEG).astype(jnp.float32)
    tok_count = jnp.take_along_axis(counts, segments, axis=1)
    scaled = (grad_out.reshape(groups, SEQ, D).astype(jnp.float32) / tok_count[:, :, None]).astype(jnp.bfloat16)
    squares = lax.map(group_squares, (hidden.reshape(groups, SEQ, FFW), scaled, segments))
    norms = jnp.sqrt(squares + EPSILON)
    factors = jnp.minimum(1.0, clip_bound() / norms)
    tok_factor = jnp.take_along_axis(factors, segments, axis=1)
    weighted = (scaled.astype(jnp.float32) * tok_factor[:, :, None]).astype(jnp.bfloat16).reshape(TOKENS, D)
    summed = lax.dot_general(weighted.astype(jnp.float32), hidden.astype(jnp.float32), (((0,), (0,)), ((), ())), precision=lax.Precision.HIGHEST)
    weight_grad = (summed + added_noise.astype(jnp.float32)).astype(jnp.bfloat16)
    return (weight_grad, norms.reshape(EXAMPLES))
```

```python
import functools
import math

import jax
import jax.numpy as jnp
from jax import lax
from jax.experimental import pallas as pl
from jax.experimental.pallas import tpu as pltpu
from jax.sharding import PartitionSpec as P

D = 4608
FFW = 18432
SEQ = 128
NSEG = 8
CORES = 2

EPSILON = 1e-06
CLIP_FRACTION = 4.2
MESH = pl.DeviceIdType.MESH
EARLY = 2


def clip_bound():
    return CLIP_FRACTION * (FFW * D * NSEG / SEQ) ** 0.5


def rows_of(index, count):
    return pl.ds(pl.multiple_of(index * count, count), count)


def kernel(
    ndp, nt, width, share, ids_ref, hid_ref, grad_ref, noise_ref, out_ref, norms_ref,
    hall, g, gt, gt_in, wt, buf, sq_t, sq_d,
    load_sem, own_send, fwd_send, mate_send, hid_recv, gt_send, gt_recv,
    share_send, share_recv, sqt_send, sqt_recv, sqd_send, sqd_recv, out_sem,
):
    d = lax.axis_index("dp")
    t = lax.axis_index("tensor")
    nz = ndp // CORES
    z = lax.div(d, CORES)
    c = lax.rem(d, CORES)
    mate = d + 1 - 2 * c
    rows, cols = buf.shape
    nk = cols // width
    part = rows // share

    def remote(src, dst, send, recv, device):
        return pltpu.make_async_remote_copy(
            src_ref=src, dst_ref=dst, send_sem=send, recv_sem=recv, device_id=device, device_id_type=MESH
        )

    def others(count, me, body):
        def step(i, carry):
            body(lax.rem(me + i, count))
            return carry

        lax.fori_loop(1, count, step, 0)

    def repeat(low, high, body):
        def step(i, carry):
            body(i)
            return carry

        lax.fori_loop(low, high, step, 0)

    load_h = pltpu.make_async_copy(hid_ref, hall.at[rows_of(d, SEQ), :], load_sem.at[0])
    load_g = pltpu.make_async_copy(grad_ref, g, load_sem.at[1])
    load_n = pltpu.make_async_copy(noise_ref, buf, load_sem.at[2])
    load_h.start()
    load_g.start()

    barrier = pltpu.get_barrier_semaphore()
    others(ndp, d, lambda j: pl.semaphore_signal(barrier, inc=1, device_id={"dp": j}, device_id_type=MESH))
    others(nt, t, lambda m: pl.semaphore_signal(barrier, inc=1, device_id={"tensor": m}, device_id_type=MESH))
    load_h.wait()
    pl.semaphore_wait(barrier, ndp + nt - 2)

    def chunk(j, k):
        return hall.at[rows_of(j, SEQ), rows_of(k, width)]

    def to(j, k, send, device):
        return remote(chunk(j, k), chunk(j, k), send, hid_recv.at[j, k], {"dp": device})

    def send_own(k):
        @pl.when(z + 1 < nz)
        def _():
            to(d, k, own_send.at[0], d + CORES).start()

        @pl.when(z > 0)
        def _():
            to(d, k, own_send.at[1], d - CORES).start()

        to(d, k, mate_send.at[z], mate).start()

    repeat(0, EARLY, send_own)

    load_g.wait()

    def turn(i):
        gt[rows_of(i, SEQ), :] = g[:, rows_of(i, SEQ)].T

    repeat(0, D // SEQ, turn)
    piece = (t if share > 1 else 0) * part

    def gt_copy(j, src_seq):
        return remote(
            gt.at[pl.ds(pl.multiple_of(j * rows + piece, 16), part), :],
            gt_in.at[src_seq, pl.ds(pl.multiple_of(piece, 16), part), :],
            gt_send.at[j], gt_recv.at[src_seq], {"dp": j},
        )

    others(ndp, d, lambda j: gt_copy(j, d).start())
    gt_in[d, pl.ds(pl.multiple_of(piece, 16), part), :] = gt[pl.ds(pl.multiple_of(d * rows + piece, 16), part), :]
    repeat(EARLY, nk, send_own)
    load_n.start()

    def members(j):
        ids = ids_ref[pl.ds(j, 1), :]
        inside = (lax.broadcasted_iota(jnp.int32, (NSEG, SEQ), 0) == ids).astype(jnp.float32)
        return ids, inside, jnp.sum(inside, axis=1, keepdims=True)

    ids, inside, count = members(d)
    contract = (((1,), (1,)), ((), ()))
    own = hall[rows_of(d, SEQ), :]
    gram_hidden = lax.dot_general(own, own, contract, preferred_element_type=jnp.float32)
    gram_raw = lax.dot_general(g[...], g[...], contract, preferred_element_type=jnp.float32)
    wide = jnp.broadcast_to(ids.astype(jnp.float32), (SEQ, SEQ))
    pairs = jnp.where(wide == wide.T, gram_hidden * gram_raw, 0.0)
    per_token = jnp.sum(pairs, axis=0, keepdims=True)
    partial = jnp.sum(inside * per_token, axis=1, keepdims=True)
    sq_t[t] = jnp.broadcast_to(partial, (NSEG, SEQ))

    def sqt_copy(m, src):
        return remote(sq_t.at[src], sq_t.at[src], sqt_send.at[m], sqt_recv.at[src], {"tensor": m})

    others(nt, t, lambda m: sqt_copy(m, t).start())
    others(nt, t, lambda m: sqt_copy(m, m).wait_recv())
    total = sq_t[0]
    for m in range(1, nt):
        total = total + sq_t[m]
    total = total / (count * count)
    sq_d[d] = total
    norms_ref[...] = jnp.sqrt(total + EPSILON)

    def sqd_copy(j, src):
        return remote(sq_d.at[src], sq_d.at[src], sqd_send.at[j], sqd_recv.at[src], {"dp": j})

    others(ndp, d, lambda j: sqd_copy(j, d).start())

    def forward(h, k):
        for way in (1, -1):
            far = z + way * h
            ahead = z - way

            @pl.when((far >= 0) & (far < nz))
            def _():
                j = far * CORES + c
                to(j, k, mate_send.at[far], mate).wait_recv()

                @pl.when((ahead >= 0) & (ahead < nz))
                def _():
                    to(j, k, fwd_send.at[far], ahead * CORES + c).start()

                to(j, k, mate_send.at[far], mate).start()

    repeat(0, nk, lambda k: forward(1, k))

    others(ndp, d, lambda j: gt_copy(j, j).wait_recv())

    def share_copy(m, src):
        block = gt_in.at[:, pl.ds(pl.multiple_of(src * part, 16), part), :]
        return remote(block, block, share_send.at[m], share_recv.at[src], {"tensor": m})

    if share > 1:
        others(nt, t, lambda m: share_copy(m, t).start())
    repeat(nk, nk * (nz - 2), lambda i: forward(1 + lax.div(i, nk), lax.rem(i, nk)))
    if share > 1:
        others(nt, t, lambda m: share_copy(m, m).wait_recv())
    others(ndp, d, lambda j: sqd_copy(j, j).wait_recv())

    def weigh(j):
        _, inside, count = members(j)
        norm = jnp.sqrt(sq_d[j] + EPSILON)
        factor = jnp.minimum(1.0, clip_bound() / norm)
        tok_count = jnp.sum(inside * count, axis=0, keepdims=True)
        tok_factor = jnp.sum(inside * factor, axis=0, keepdims=True)
        scaled = (gt_in[j].astype(jnp.float32) / tok_count).astype(jnp.bfloat16)
        wt[:, rows_of(j, SEQ)] = (scaled.astype(jnp.float32) * tok_factor).astype(jnp.bfloat16)

    repeat(0, ndp, weigh)
    load_n.wait()

    def out_copy(k):
        return pltpu.make_async_copy(
            buf.at[:, rows_of(k, width)], out_ref.at[:, rows_of(k, width)], out_sem.at[k]
        )

    def multiply(k):
        repeat(0, nz, lambda far: to(far * CORES + 1 - c, k, mate_send.at[far], mate).wait_recv())
        at = rows_of(k, width)
        summed = jnp.dot(wt[...], hall[:, at], preferred_element_type=jnp.float32)
        buf[:, at] = (summed + buf[:, at].astype(jnp.float32)).astype(jnp.bfloat16)
        out_copy(k).start()

    def last(k):
        @pl.when(k < nk)
        def _():
            forward(nz - 1, k)

        @pl.when(k > 0)
        def _():
            multiply(k - 1)

    repeat(0, nk + 1, last)

    def sent(far, sem):
        block = hall.at[rows_of(far * CORES + c, SEQ), :]
        remote(block, block, sem, hid_recv.at[0, 0], {"dp": mate}).wait_send()

    @pl.when(z + 1 < nz)
    def _():
        sent(z, own_send.at[0])

    @pl.when(z > 0)
    def _():
        sent(z, own_send.at[1])

    repeat(0, nz, lambda far: sent(far, mate_send.at[far]))

    def sent_on(far):
        inner = (z > 0) & (z < nz - 1) & (far != z)

        @pl.when(inner)
        def _():
            sent(far, fwd_send.at[far])

    repeat(0, nz, sent_on)
    others(ndp, d, lambda j: gt_copy(j, d).wait_send())
    others(ndp, d, lambda j: sqd_copy(j, d).wait_send())
    others(nt, t, lambda m: sqt_copy(m, t).wait_send())
    if share > 1:
        others(nt, t, lambda m: share_copy(m, t).wait_send())
    repeat(0, nk, lambda k: out_copy(k).wait())


def per_device(ndp, nt, hidden, grad_out, seg_ids, seg_counts, added_noise):
    rows, cols = added_noise.shape
    width = next(w for w in (512, 384, 256, 128) if cols % w == 0)
    share = nt if rows % (16 * nt) == 0 else 1
    nz = ndp // CORES
    nk = cols // width
    dma = pltpu.SemaphoreType.DMA
    anywhere = pl.BlockSpec(memory_space=pl.ANY)
    vmem = pl.BlockSpec(memory_space=pltpu.VMEM)
    out, norms = pl.pallas_call(
        functools.partial(kernel, ndp, nt, width, share),
        out_shape=(
            jax.ShapeDtypeStruct((rows, cols), jnp.bfloat16),
            jax.ShapeDtypeStruct((NSEG, SEQ), jnp.float32),
        ),
        in_specs=[vmem, anywhere, anywhere, anywhere],
        out_specs=(anywhere, vmem),
        scratch_shapes=[
            pltpu.VMEM((ndp * SEQ, cols), jnp.bfloat16),
            pltpu.VMEM((SEQ, D), jnp.bfloat16),
            pltpu.VMEM((D, SEQ), jnp.bfloat16),
            pltpu.VMEM((ndp, rows, SEQ), jnp.bfloat16),
            pltpu.VMEM((rows, ndp * SEQ), jnp.bfloat16),
            pltpu.VMEM((rows, cols), jnp.bfloat16),
            pltpu.VMEM((nt, NSEG, SEQ), jnp.float32),
            pltpu.VMEM((ndp, NSEG, SEQ), jnp.float32),
            dma((3,)), dma((2,)), dma((nz,)), dma((nz,)), dma((ndp, nk)), dma((ndp,)), dma((ndp,)),
            dma((nt,)), dma((nt,)), dma((nt,)), dma((nt,)), dma((ndp,)), dma((ndp,)), dma((nk,)),
        ],
        compiler_params=pltpu.CompilerParams(
            collective_id=0, has_side_effects=True, vmem_limit_bytes=48 * 1024 * 1024
        ),
        cost_estimate=pl.CostEstimate(
            flops=2 * ndp * SEQ * rows * cols, bytes_accessed=4 * rows * cols, transcendentals=0
        ),
    )(seg_ids.reshape(ndp, SEQ), hidden, grad_out, added_noise)
    return out, norms[:, 0]


def solution(mesh):
    placed = (P("dp", "tensor"), P("dp", None), P(), P("dp"), P("dp", "tensor"))
    return jax.shard_map(
        functools.partial(per_device, mesh.shape["dp"], mesh.shape["tensor"]),
        mesh=mesh,
        in_specs=placed,
        out_specs=(P("dp", "tensor"), P("dp")),
        check_vma=False,
    )
```

```python
import functools
import math

import jax
import jax.numpy as jnp
from jax import lax
from jax.experimental import pallas as pl
from jax.experimental.pallas import tpu as pltpu
from jax.sharding import PartitionSpec as P

D = 4608
FFW = 18432
SEQ = 128
NSEG = 8
CORES = 2

EPSILON = 1e-06
CLIP_FRACTION = 4.2
MESH = pl.DeviceIdType.MESH
EARLY = 3


def clip_bound():
    return CLIP_FRACTION * (FFW * D * NSEG / SEQ) ** 0.5


def rows_of(index, count):
    return pl.ds(pl.multiple_of(index * count, count), count)


def kernel(
    ndp, nt, width, share, ids_in, hid_ref, grad_ref, noise_ref, out_ref, norms_ref,
    ids_ref, hall, g, gt, gt_in, wt, sq_t, sq_d,
    load_sem, own_send, fwd_send, mate_send, hid_recv, gt_send, gt_recv,
    share_send, share_recv, sqt_send, sqt_recv, sqd_send, sqd_recv,
):
    d = lax.axis_index("dp")
    t = lax.axis_index("tensor")
    nz = ndp // CORES
    z = lax.div(d, CORES)
    c = lax.rem(d, CORES)
    mate = d + 1 - 2 * c
    rows, cols = out_ref.shape
    nk = cols // width
    part = rows // share

    def remote(src, dst, send, recv, device):
        return pltpu.make_async_remote_copy(
            src_ref=src, dst_ref=dst, send_sem=send, recv_sem=recv, device_id=device, device_id_type=MESH
        )

    def others(count, me, body):
        def step(i, carry):
            body(lax.rem(me + i, count))
            return carry

        lax.fori_loop(1, count, step, 0)

    def repeat(low, high, body):
        def step(i, carry):
            body(i)
            return carry

        lax.fori_loop(low, high, step, 0)

    load_h = pltpu.make_async_copy(hid_ref, hall.at[rows_of(d, SEQ), :], load_sem.at[0])
    load_g = pltpu.make_async_copy(grad_ref, g, load_sem.at[1])
    load_n = pltpu.make_async_copy(noise_ref, out_ref, load_sem.at[2])
    load_i = pltpu.make_async_copy(ids_in, ids_ref, load_sem.at[3])
    load_h.start()
    load_g.start()
    load_i.start()

    barrier = pltpu.get_barrier_semaphore()
    others(ndp, d, lambda j: pl.semaphore_signal(barrier, inc=1, device_id={"dp": j}, device_id_type=MESH))
    others(nt, t, lambda m: pl.semaphore_signal(barrier, inc=1, device_id={"tensor": m}, device_id_type=MESH))
    load_h.wait()
    pl.semaphore_wait(barrier, ndp + nt - 2)

    def chunk(j, k):
        return hall.at[rows_of(j, SEQ), rows_of(k, width)]

    def to(j, k, send, device):
        return remote(chunk(j, k), chunk(j, k), send, hid_recv.at[j, k], {"dp": device})

    def send_own(k):
        @pl.when(z + 1 < nz)
        def _():
            to(d, k, own_send.at[0], d + CORES).start()

        @pl.when(z > 0)
        def _():
            to(d, k, own_send.at[1], d - CORES).start()

        to(d, k, mate_send.at[z], mate).start()

    repeat(0, EARLY, send_own)

    load_g.wait()

    def turn(i):
        gt[rows_of(i, SEQ), :] = g[:, rows_of(i, SEQ)].T

    repeat(0, D // SEQ, turn)
    piece = (t if share > 1 else 0) * part

    def gt_copy(j, src_seq):
        return remote(
            gt.at[pl.ds(pl.multiple_of(j * rows + piece, 16), part), :],
            gt_in.at[src_seq, pl.ds(pl.multiple_of(piece, 16), part), :],
            gt_send.at[j], gt_recv.at[src_seq], {"dp": j},
        )

    others(ndp, d, lambda j: gt_copy(j, d).start())
    gt_in[d, pl.ds(pl.multiple_of(piece, 16), part), :] = gt[pl.ds(pl.multiple_of(d * rows + piece, 16), part), :]
    repeat(EARLY, nk, send_own)
    load_n.start()

    def members(j):
        ids = ids_ref[pl.ds(j, 1), :]
        inside = (lax.broadcasted_iota(jnp.int32, (NSEG, SEQ), 0) == ids).astype(jnp.float32)
        return ids, inside, jnp.sum(inside, axis=1, keepdims=True)

    load_i.wait()
    ids, inside, count = members(d)
    contract = (((1,), (1,)), ((), ()))
    own = hall[rows_of(d, SEQ), :]
    gram_hidden = lax.dot_general(own, own, contract, preferred_element_type=jnp.float32)
    gram_raw = lax.dot_general(g[...], g[...], contract, preferred_element_type=jnp.float32)
    wide = jnp.broadcast_to(ids.astype(jnp.float32), (SEQ, SEQ))
    pairs = jnp.where(wide == wide.T, gram_hidden * gram_raw, 0.0)
    per_token = jnp.sum(pairs, axis=0, keepdims=True)
    partial = jnp.sum(inside * per_token, axis=1, keepdims=True)
    sq_t[t] = jnp.broadcast_to(partial, (NSEG, SEQ))

    def sqt_copy(m, src):
        return remote(sq_t.at[src], sq_t.at[src], sqt_send.at[m], sqt_recv.at[src], {"tensor": m})

    others(nt, t, lambda m: sqt_copy(m, t).start())
    others(nt, t, lambda m: sqt_copy(m, m).wait_recv())
    total = sq_t[0]
    for m in range(1, nt):
        total = total + sq_t[m]
    total = total / (count * count)
    sq_d[d] = total
    norms_ref[...] = jnp.sqrt(total + EPSILON)[:, 0]

    def sqd_copy(j, src):
        return remote(sq_d.at[src], sq_d.at[src], sqd_send.at[j], sqd_recv.at[src], {"dp": j})

    others(ndp, d, lambda j: sqd_copy(j, d).start())

    def forward(h, k):
        for way in (1, -1):
            far = z + way * h
            ahead = z - way

            @pl.when((far >= 0) & (far < nz))
            def _():
                j = far * CORES + c
                to(j, k, mate_send.at[far], mate).wait_recv()

                @pl.when((ahead >= 0) & (ahead < nz))
                def _():
                    to(j, k, fwd_send.at[far], ahead * CORES + c).start()

                to(j, k, mate_send.at[far], mate).start()

    repeat(0, nk, lambda k: forward(1, k))

    others(ndp, d, lambda j: gt_copy(j, j).wait_recv())

    def share_copy(m, src):
        block = gt_in.at[:, pl.ds(pl.multiple_of(src * part, 16), part), :]
        return remote(block, block, share_send.at[m], share_recv.at[src], {"tensor": m})

    if share > 1:
        others(nt, t, lambda m: share_copy(m, t).start())
    repeat(nk, nk * (nz - 2), lambda i: forward(1 + lax.div(i, nk), lax.rem(i, nk)))
    if share > 1:
        others(nt, t, lambda m: share_copy(m, m).wait_recv())
    others(ndp, d, lambda j: sqd_copy(j, j).wait_recv())

    def weigh(j):
        _, inside, count = members(j)
        norm = jnp.sqrt(sq_d[j] + EPSILON)
        factor = jnp.minimum(1.0, clip_bound() / norm)
        tok_count = jnp.sum(inside * count, axis=0, keepdims=True)
        tok_factor = jnp.sum(inside * factor, axis=0, keepdims=True)
        scaled = (gt_in[j].astype(jnp.float32) / tok_count).astype(jnp.bfloat16)
        wt[:, rows_of(j, SEQ)] = (scaled.astype(jnp.float32) * tok_factor).astype(jnp.bfloat16)

    def sent(far, sem):
        block = hall.at[rows_of(far * CORES + c, SEQ), :]
        remote(block, block, sem, hid_recv.at[0, 0], {"dp": mate}).wait_send()

    @pl.when(z + 1 < nz)
    def _():
        sent(z, own_send.at[0])

    @pl.when(z > 0)
    def _():
        sent(z, own_send.at[1])

    sent(z, mate_send.at[z])
    others(ndp, d, lambda j: gt_copy(j, d).wait_send())
    others(ndp, d, lambda j: sqd_copy(j, d).wait_send())
    others(nt, t, lambda m: sqt_copy(m, t).wait_send())
    if share > 1:
        others(nt, t, lambda m: share_copy(m, t).wait_send())
    repeat(0, ndp, weigh)
    load_n.wait()

    def multiply(k):
        repeat(0, nz, lambda far: to(far * CORES + 1 - c, k, mate_send.at[far], mate).wait_recv())
        at = rows_of(k, width)
        summed = jnp.dot(wt[...], hall[:, at], preferred_element_type=jnp.float32)
        out_ref[:, at] = (summed + out_ref[:, at].astype(jnp.float32)).astype(jnp.bfloat16)

    def last(k):
        @pl.when(k < nk)
        def _():
            forward(nz - 1, k)

        @pl.when(k > 0)
        def _():
            multiply(k - 1)

    repeat(0, nk + 1, last)

    def sent_on(far):
        @pl.when(far != z)
        def _():
            sent(far, mate_send.at[far])

        @pl.when((z > 0) & (z < nz - 1) & (far != z))
        def _():
            sent(far, fwd_send.at[far])

    repeat(0, nz, sent_on)


def per_device(ndp, nt, hidden, grad_out, seg_ids, seg_counts, added_noise):
    rows, cols = added_noise.shape
    width = next(w for w in (256, 384, 128) if cols % w == 0)
    share = nt if rows % (16 * nt) == 0 else 1
    nz = ndp // CORES
    nk = cols // width
    dma = pltpu.SemaphoreType.DMA
    hbm = pl.BlockSpec(memory_space=pltpu.HBM)
    vmem = pl.BlockSpec(memory_space=pltpu.VMEM)
    out, norms = pl.pallas_call(
        functools.partial(kernel, ndp, nt, width, share),
        out_shape=(
            jax.ShapeDtypeStruct((rows, cols), jnp.bfloat16),
            jax.ShapeDtypeStruct((NSEG,), jnp.float32),
        ),
        in_specs=[hbm] * 4,
        out_specs=(vmem, vmem),
        scratch_shapes=[
            pltpu.VMEM((ndp, SEQ), jnp.int32),
            pltpu.VMEM((ndp * SEQ, cols), jnp.bfloat16),
            pltpu.VMEM((SEQ, D), jnp.bfloat16),
            pltpu.VMEM((D, SEQ), jnp.bfloat16),
            pltpu.VMEM((ndp, rows, SEQ), jnp.bfloat16),
            pltpu.VMEM((rows, ndp * SEQ), jnp.bfloat16),
            pltpu.VMEM((nt, NSEG, SEQ), jnp.float32),
            pltpu.VMEM((ndp, NSEG, SEQ), jnp.float32),
            dma((4,)), dma((2,)), dma((nz,)), dma((nz,)), dma((ndp, nk)), dma((ndp,)), dma((ndp,)),
            dma((nt,)), dma((nt,)), dma((nt,)), dma((nt,)), dma((ndp,)), dma((ndp,)),
        ],
        compiler_params=pltpu.CompilerParams(
            collective_id=0, has_side_effects=True, vmem_limit_bytes=32 * 1024 * 1024
        ),
        cost_estimate=pl.CostEstimate(
            flops=2 * ndp * SEQ * rows * cols, bytes_accessed=4 * rows * cols, transcendentals=0
        ),
    )(
        *(
            pltpu.with_memory_space_constraint(x, pltpu.HBM)
            for x in (seg_ids.reshape(ndp, SEQ), hidden, grad_out, added_noise)
        )
    )
    return out, norms


def solution(mesh):
    placed = (P("dp", "tensor"), P("dp", None), P(), P("dp"), P("dp", "tensor"))
    return jax.shard_map(
        functools.partial(per_device, mesh.shape["dp"], mesh.shape["tensor"]),
        mesh=mesh,
        in_specs=placed,
        out_specs=(P("dp", "tensor"), P("dp")),
        check_vma=False,
    )
```

```python
import functools
import math

import jax
import jax.numpy as jnp
from jax import lax
from jax.experimental import pallas as pl
from jax.experimental.pallas import tpu as pltpu
from jax.sharding import PartitionSpec as P

D = 4608
FFW = 18432
SEQ = 128
NSEG = 8
CORES = 2

EPSILON = 1e-06
CLIP_FRACTION = 4.2
MESH = pl.DeviceIdType.MESH
EARLY = 3


def clip_bound():
    return CLIP_FRACTION * (FFW * D * NSEG / SEQ) ** 0.5


def rows_of(index, count):
    return pl.ds(pl.multiple_of(index * count, count), count)


def kernel(
    ndp, nt, width, share, ids_in, hid_ref, grad_ref, noise_ref, out_ref, norms_ref,
    ids_ref, hall, g, gt, gt_in, wt, sq_t, sq_d,
    load_sem, hid_load, own_send, fwd_send, mate_send, hid_recv, gt_send, gt_recv,
    share_send, share_recv, sqt_send, sqt_recv, sqd_send, sqd_recv,
):
    d = lax.axis_index("dp")
    t = lax.axis_index("tensor")
    nz = ndp // CORES
    z = lax.div(d, CORES)
    c = lax.rem(d, CORES)
    mate = d + 1 - 2 * c
    rows, cols = out_ref.shape
    nk = cols // width
    part = rows // share

    def remote(src, dst, send, recv, device):
        return pltpu.make_async_remote_copy(
            src_ref=src, dst_ref=dst, send_sem=send, recv_sem=recv, device_id=device, device_id_type=MESH
        )

    def others(count, me, body):
        def step(i, carry):
            body(lax.rem(me + i, count))
            return carry

        lax.fori_loop(1, count, step, 0)

    def repeat(low, high, body):
        def step(i, carry):
            body(i)
            return carry

        lax.fori_loop(low, high, step, 0)

    def load_h(k):
        return pltpu.make_async_copy(
            hid_ref.at[:, rows_of(k, width)], hall.at[k, rows_of(d, SEQ), :], hid_load.at[k]
        )

    load_g = pltpu.make_async_copy(grad_ref, g, load_sem.at[0])
    load_n = pltpu.make_async_copy(noise_ref, out_ref, load_sem.at[1])
    load_i = pltpu.make_async_copy(ids_in, ids_ref, load_sem.at[2])
    repeat(0, nk, lambda k: load_h(k).start())
    load_g.start()
    load_i.start()

    barrier = pltpu.get_barrier_semaphore()
    others(ndp, d, lambda j: pl.semaphore_signal(barrier, inc=1, device_id={"dp": j}, device_id_type=MESH))
    others(nt, t, lambda m: pl.semaphore_signal(barrier, inc=1, device_id={"tensor": m}, device_id_type=MESH))
    pl.semaphore_wait(barrier, ndp + nt - 2)

    def chunk(j, k):
        return hall.at[k, rows_of(j, SEQ), :]

    def to(j, k, send, device):
        return remote(chunk(j, k), chunk(j, k), send, hid_recv.at[j, k], {"dp": device})

    def send_own(k):
        load_h(k).wait()

        @pl.when(z + 1 < nz)
        def _():
            to(d, k, own_send.at[0], d + CORES).start()

        @pl.when(z > 0)
        def _():
            to(d, k, own_send.at[1], d - CORES).start()

        to(d, k, mate_send.at[z], mate).start()

    repeat(0, EARLY, send_own)

    load_g.wait()

    def turn(i):
        gt[rows_of(i, SEQ), :] = g[:, rows_of(i, SEQ)].T

    repeat(0, D // SEQ, turn)
    piece = (t if share > 1 else 0) * part

    def gt_copy(j, src_seq):
        return remote(
            gt.at[pl.ds(pl.multiple_of(j * rows + piece, 16), part), :],
            gt_in.at[src_seq, pl.ds(pl.multiple_of(piece, 16), part), :],
            gt_send.at[j], gt_recv.at[src_seq], {"dp": j},
        )

    others(ndp, d, lambda j: gt_copy(j, d).start())
    gt_in[d, pl.ds(pl.multiple_of(piece, 16), part), :] = gt[pl.ds(pl.multiple_of(d * rows + piece, 16), part), :]
    repeat(EARLY, nk, send_own)
    load_n.start()

    def members(j):
        ids = ids_ref[pl.ds(j, 1), :]
        inside = (lax.broadcasted_iota(jnp.int32, (NSEG, SEQ), 0) == ids).astype(jnp.float32)
        return ids, inside, jnp.sum(inside, axis=1, keepdims=True)

    load_i.wait()
    ids, inside, count = members(d)
    contract = (((1,), (1,)), ((), ()))

    def gram(k, held):
        own = hall[k, rows_of(d, SEQ), :]
        return held + lax.dot_general(own, own, contract, preferred_element_type=jnp.float32)

    gram_hidden = lax.fori_loop(0, nk, gram, jnp.zeros((SEQ, SEQ), jnp.float32))
    gram_raw = lax.dot_general(g[...], g[...], contract, preferred_element_type=jnp.float32)
    wide = jnp.broadcast_to(ids.astype(jnp.float32), (SEQ, SEQ))
    pairs = jnp.where(wide == wide.T, gram_hidden * gram_raw, 0.0)
    per_token = jnp.sum(pairs, axis=0, keepdims=True)
    partial = jnp.sum(inside * per_token, axis=1, keepdims=True)
    sq_t[t] = jnp.broadcast_to(partial, (NSEG, SEQ))

    def sqt_copy(m, src):
        return remote(sq_t.at[src], sq_t.at[src], sqt_send.at[m], sqt_recv.at[src], {"tensor": m})

    others(nt, t, lambda m: sqt_copy(m, t).start())
    others(nt, t, lambda m: sqt_copy(m, m).wait_recv())
    total = sq_t[0]
    for m in range(1, nt):
        total = total + sq_t[m]
    total = total / (count * count)
    sq_d[d] = total
    norms_ref[...] = jnp.sqrt(total + EPSILON)[:, 0]

    def sqd_copy(j, src):
        return remote(sq_d.at[src], sq_d.at[src], sqd_send.at[j], sqd_recv.at[src], {"dp": j})

    others(ndp, d, lambda j: sqd_copy(j, d).start())

    def forward(h, k):
        for way in (1, -1):
            far = z + way * h
            ahead = z - way

            @pl.when((far >= 0) & (far < nz))
            def _():
                j = far * CORES + c
                to(j, k, mate_send.at[far], mate).wait_recv()

                @pl.when((ahead >= 0) & (ahead < nz))
                def _():
                    to(j, k, fwd_send.at[far], ahead * CORES + c).start()

                to(j, k, mate_send.at[far], mate).start()

    repeat(0, nk, lambda k: forward(1, k))

    others(ndp, d, lambda j: gt_copy(j, j).wait_recv())

    def share_copy(m, src):
        block = gt_in.at[:, pl.ds(pl.multiple_of(src * part, 16), part), :]
        return remote(block, block, share_send.at[m], share_recv.at[src], {"tensor": m})

    if share > 1:
        others(nt, t, lambda m: share_copy(m, t).start())
    repeat(nk, nk * (nz - 2), lambda i: forward(1 + lax.div(i, nk), lax.rem(i, nk)))
    if share > 1:
        others(nt, t, lambda m: share_copy(m, m).wait_recv())
    others(ndp, d, lambda j: sqd_copy(j, j).wait_recv())

    def weigh(j):
        _, inside, count = members(j)
        norm = jnp.sqrt(sq_d[j] + EPSILON)
        factor = jnp.minimum(1.0, clip_bound() / norm)
        tok_count = jnp.sum(inside * count, axis=0, keepdims=True)
        tok_factor = jnp.sum(inside * factor, axis=0, keepdims=True)
        scaled = (gt_in[j].astype(jnp.float32) / tok_count).astype(jnp.bfloat16)
        wt[:, rows_of(j, SEQ)] = (scaled.astype(jnp.float32) * tok_factor).astype(jnp.bfloat16)

    def sent(far, sem):
        block = hall.at[:, rows_of(far * CORES + c, SEQ), :]
        remote(block, block, sem, hid_recv.at[0, 0], {"dp": mate}).wait_send()

    @pl.when(z + 1 < nz)
    def _():
        sent(z, own_send.at[0])

    @pl.when(z > 0)
    def _():
        sent(z, own_send.at[1])

    sent(z, mate_send.at[z])
    others(ndp, d, lambda j: gt_copy(j, d).wait_send())
    others(ndp, d, lambda j: sqd_copy(j, d).wait_send())
    others(nt, t, lambda m: sqt_copy(m, t).wait_send())
    if share > 1:
        others(nt, t, lambda m: share_copy(m, t).wait_send())
    repeat(0, ndp, weigh)
    load_n.wait()

    def multiply(k):
        repeat(0, nz, lambda far: to(far * CORES + 1 - c, k, mate_send.at[far], mate).wait_recv())
        at = rows_of(k, width)
        summed = jnp.dot(wt[...], hall[k], preferred_element_type=jnp.float32)
        out_ref[:, at] = (summed + out_ref[:, at].astype(jnp.float32)).astype(jnp.bfloat16)

    def last(k):
        @pl.when(k < nk)
        def _():
            forward(nz - 1, k)

        @pl.when(k > 0)
        def _():
            multiply(k - 1)

    repeat(0, nk + 1, last)

    def sent_on(far):
        @pl.when(far != z)
        def _():
            sent(far, mate_send.at[far])

        @pl.when((z > 0) & (z < nz - 1) & (far != z))
        def _():
            sent(far, fwd_send.at[far])

    repeat(0, nz, sent_on)


def place(pieces, held_ref, held_norms_ref, out_ref, norms_ref, sem):
    part = out_ref.shape[0] // pieces
    copies = [pltpu.make_async_copy(held_norms_ref, norms_ref, sem.at[pieces])]
    for i in range(pieces):
        at = pl.ds(i * part, part)
        copies.append(pltpu.make_async_copy(held_ref.at[at, :], out_ref.at[at, :], sem.at[i]))
    for copy in copies:
        copy.start()
    for copy in copies:
        copy.wait()


def per_device(ndp, nt, hidden, grad_out, seg_ids, seg_counts, added_noise):
    rows, cols = added_noise.shape
    width = next(w for w in (256, 384, 128) if cols % w == 0)
    share = nt if rows % (16 * nt) == 0 else 1
    nz = ndp // CORES
    nk = cols // width
    dma = pltpu.SemaphoreType.DMA
    hbm = pl.BlockSpec(memory_space=pltpu.HBM)
    vmem = pl.BlockSpec(memory_space=pltpu.VMEM)
    out, norms = pl.pallas_call(
        functools.partial(kernel, ndp, nt, width, share),
        out_shape=(
            jax.ShapeDtypeStruct((rows, cols), jnp.bfloat16),
            jax.ShapeDtypeStruct((NSEG,), jnp.float32),
        ),
        in_specs=[hbm] * 4,
        out_specs=(vmem, vmem),
        scratch_shapes=[
            pltpu.VMEM((ndp, SEQ), jnp.int32),
            pltpu.VMEM((nk, ndp * SEQ, width), jnp.bfloat16),
            pltpu.VMEM((SEQ, D), jnp.bfloat16),
            pltpu.VMEM((D, SEQ), jnp.bfloat16),
            pltpu.VMEM((ndp, rows, SEQ), jnp.bfloat16),
            pltpu.VMEM((rows, ndp * SEQ), jnp.bfloat16),
            pltpu.VMEM((nt, NSEG, SEQ), jnp.float32),
            pltpu.VMEM((ndp, NSEG, SEQ), jnp.float32),
            dma((3,)), dma((nk,)), dma((2,)), dma((nz,)), dma((nz,)), dma((ndp, nk)), dma((ndp,)), dma((ndp,)),
            dma((nt,)), dma((nt,)), dma((nt,)), dma((nt,)), dma((ndp,)), dma((ndp,)),
        ],
        compiler_params=pltpu.CompilerParams(
            collective_id=0, has_side_effects=True, vmem_limit_bytes=32 * 1024 * 1024
        ),
        cost_estimate=pl.CostEstimate(
            flops=2 * ndp * SEQ * rows * cols, bytes_accessed=4 * rows * cols, transcendentals=0
        ),
    )(
        *(
            pltpu.with_memory_space_constraint(x, pltpu.HBM)
            for x in (seg_ids.reshape(ndp, SEQ), hidden, grad_out, added_noise)
        )
    )
    pieces = 8 if rows % 128 == 0 else 9
    return pl.pallas_call(
        functools.partial(place, pieces),
        out_shape=(
            jax.ShapeDtypeStruct((rows, cols), jnp.bfloat16),
            jax.ShapeDtypeStruct((NSEG,), jnp.float32),
        ),
        in_specs=[pl.BlockSpec(memory_space=pl.ANY)] * 2,
        out_specs=(pl.BlockSpec(memory_space=pl.ANY),) * 2,
        scratch_shapes=[dma((pieces + 1,))],
        compiler_params=pltpu.CompilerParams(vmem_limit_bytes=1024 * 1024),
        cost_estimate=pl.CostEstimate(flops=0, bytes_accessed=4 * rows * cols, transcendentals=0),
    )(out, norms)


def solution(mesh):
    placed = (P("dp", "tensor"), P("dp", None), P(), P("dp"), P("dp", "tensor"))
    return jax.shard_map(
        functools.partial(per_device, mesh.shape["dp"], mesh.shape["tensor"]),
        mesh=mesh,
        in_specs=placed,
        out_specs=(P("dp", "tensor"), P("dp")),
        check_vma=False,
    )
```

```python
import functools
import math

import jax
import jax.numpy as jnp
from jax import lax
from jax.experimental import pallas as pl
from jax.experimental.pallas import tpu as pltpu
from jax.sharding import PartitionSpec as P

D = 4608
FFW = 18432
SEQ = 128
NSEG = 8
CORES = 2

EPSILON = 1e-06
CLIP_FRACTION = 4.2
MESH = pl.DeviceIdType.MESH
EARLY = 3


def clip_bound():
    return CLIP_FRACTION * (FFW * D * NSEG / SEQ) ** 0.5


def rows_of(index, count):
    return pl.ds(pl.multiple_of(index * count, count), count)


def kernel(
    ndp, nt, width, share, ids_in, hid_ref, grad_ref, noise_ref, out_ref, norms_ref,
    ids_ref, hall, g, gt, gt_in, wt, sq_t, sq_d,
    load_sem, hid_load, own_send, fwd_send, mate_send, hid_recv, gt_send, gt_recv,
    share_send, share_recv, sqt_send, sqt_recv, sqd_send, sqd_recv,
):
    d = lax.axis_index("dp")
    t = lax.axis_index("tensor")
    nz = ndp // CORES
    z = lax.div(d, CORES)
    c = lax.rem(d, CORES)
    mate = d + 1 - 2 * c
    rows, cols = out_ref.shape
    nk = cols // width
    part = rows // share

    def remote(src, dst, send, recv, device):
        return pltpu.make_async_remote_copy(
            src_ref=src, dst_ref=dst, send_sem=send, recv_sem=recv, device_id=device, device_id_type=MESH
        )

    def others(count, me, body):
        def step(i, carry):
            body(lax.rem(me + i, count))
            return carry

        lax.fori_loop(1, count, step, 0)

    def repeat(low, high, body):
        def step(i, carry):
            body(i)
            return carry

        lax.fori_loop(low, high, step, 0)

    def load_h(k):
        return pltpu.make_async_copy(
            hid_ref.at[:, rows_of(k, width)], hall.at[k, rows_of(d, SEQ), :], hid_load.at[k]
        )

    load_g = pltpu.make_async_copy(grad_ref, g, load_sem.at[0])
    load_n = pltpu.make_async_copy(noise_ref, out_ref, load_sem.at[1])
    load_i = pltpu.make_async_copy(ids_in, ids_ref, load_sem.at[2])
    repeat(0, nk, lambda k: load_h(k).start())
    load_g.start()
    load_i.start()

    barrier = pltpu.get_barrier_semaphore()
    others(ndp, d, lambda j: pl.semaphore_signal(barrier, inc=1, device_id={"dp": j}, device_id_type=MESH))
    others(nt, t, lambda m: pl.semaphore_signal(barrier, inc=1, device_id={"tensor": m}, device_id_type=MESH))
    pl.semaphore_wait(barrier, ndp + nt - 2)

    def chunk(j, k):
        return hall.at[k, rows_of(j, SEQ), :]

    def to(j, k, send, device):
        return remote(chunk(j, k), chunk(j, k), send, hid_recv.at[j, k], {"dp": device})

    def send_own(k):
        load_h(k).wait()

        @pl.when(z + 1 < nz)
        def _():
            to(d, k, own_send.at[0], d + CORES).start()

        @pl.when(z > 0)
        def _():
            to(d, k, own_send.at[1], d - CORES).start()

        @pl.when((z == 0) | (z == nz - 1))
        def _():
            to(d, k, own_send.at[2], (nz - 1 - z) * CORES + c).start()

        to(d, k, mate_send.at[z], mate).start()

    repeat(0, EARLY, send_own)

    load_g.wait()

    def turn(i):
        gt[rows_of(i, SEQ), :] = g[:, rows_of(i, SEQ)].T

    repeat(0, D // SEQ, turn)
    piece = (t if share > 1 else 0) * part

    def gt_copy(j, src_seq):
        return remote(
            gt.at[pl.ds(pl.multiple_of(j * rows + piece, 16), part), :],
            gt_in.at[src_seq, pl.ds(pl.multiple_of(piece, 16), part), :],
            gt_send.at[j], gt_recv.at[src_seq], {"dp": j},
        )

    others(ndp, d, lambda j: gt_copy(j, d).start())
    gt_in[d, pl.ds(pl.multiple_of(piece, 16), part), :] = gt[pl.ds(pl.multiple_of(d * rows + piece, 16), part), :]
    repeat(EARLY, nk, send_own)
    load_n.start()

    def members(j):
        ids = ids_ref[pl.ds(j, 1), :]
        inside = (lax.broadcasted_iota(jnp.int32, (NSEG, SEQ), 0) == ids).astype(jnp.float32)
        return ids, inside, jnp.sum(inside, axis=1, keepdims=True)

    load_i.wait()
    ids, inside, count = members(d)
    contract = (((1,), (1,)), ((), ()))

    def gram(k, held):
        own = hall[k, rows_of(d, SEQ), :]
        return held + lax.dot_general(own, own, contract, preferred_element_type=jnp.float32)

    gram_hidden = lax.fori_loop(0, nk, gram, jnp.zeros((SEQ, SEQ), jnp.float32))
    gram_raw = lax.dot_general(g[...], g[...], contract, preferred_element_type=jnp.float32)
    wide = jnp.broadcast_to(ids.astype(jnp.float32), (SEQ, SEQ))
    pairs = jnp.where(wide == wide.T, gram_hidden * gram_raw, 0.0)
    per_token = jnp.sum(pairs, axis=0, keepdims=True)
    partial = jnp.sum(inside * per_token, axis=1, keepdims=True)
    sq_t[t] = jnp.broadcast_to(partial, (NSEG, SEQ))

    def sqt_copy(m, src):
        return remote(sq_t.at[src], sq_t.at[src], sqt_send.at[m], sqt_recv.at[src], {"tensor": m})

    others(nt, t, lambda m: sqt_copy(m, t).start())
    others(nt, t, lambda m: sqt_copy(m, m).wait_recv())
    total = sq_t[0]
    for m in range(1, nt):
        total = total + sq_t[m]
    total = total / (count * count)
    sq_d[d] = total
    norms_ref[...] = jnp.sqrt(total + EPSILON)[:, 0]

    def sqd_copy(j, src):
        return remote(sq_d.at[src], sq_d.at[src], sqd_send.at[j], sqd_recv.at[src], {"dp": j})

    others(ndp, d, lambda j: sqd_copy(j, d).start())

    def forward(h, k):
        for way in (1, -1):
            far = z + way * h
            ahead = z - way

            @pl.when((far >= 0) & (far < nz))
            def _():
                j = far * CORES + c
                to(j, k, mate_send.at[far], mate).wait_recv()

                @pl.when((ahead >= 0) & (ahead < nz) & (h + 1 < nz - 1))
                def _():
                    to(j, k, fwd_send.at[far], ahead * CORES + c).start()

                to(j, k, mate_send.at[far], mate).start()

    repeat(0, nk, lambda k: forward(1, k))

    others(ndp, d, lambda j: gt_copy(j, j).wait_recv())

    def share_copy(m, src):
        block = gt_in.at[:, pl.ds(pl.multiple_of(src * part, 16), part), :]
        return remote(block, block, share_send.at[m], share_recv.at[src], {"tensor": m})

    if share > 1:
        others(nt, t, lambda m: share_copy(m, t).start())
    repeat(nk, nk * (nz - 3), lambda i: forward(1 + lax.div(i, nk), lax.rem(i, nk)))
    if share > 1:
        others(nt, t, lambda m: share_copy(m, m).wait_recv())
    others(ndp, d, lambda j: sqd_copy(j, j).wait_recv())

    def weigh(j):
        _, inside, count = members(j)
        norm = jnp.sqrt(sq_d[j] + EPSILON)
        factor = jnp.minimum(1.0, clip_bound() / norm)
        tok_count = jnp.sum(inside * count, axis=0, keepdims=True)
        tok_factor = jnp.sum(inside * factor, axis=0, keepdims=True)
        scaled = (gt_in[j].astype(jnp.float32) / tok_count).astype(jnp.bfloat16)
        wt[:, rows_of(j, SEQ)] = (scaled.astype(jnp.float32) * tok_factor).astype(jnp.bfloat16)

    def sent(far, sem):
        block = hall.at[:, rows_of(far * CORES + c, SEQ), :]
        remote(block, block, sem, hid_recv.at[0, 0], {"dp": mate}).wait_send()

    @pl.when(z + 1 < nz)
    def _():
        sent(z, own_send.at[0])

    @pl.when(z > 0)
    def _():
        sent(z, own_send.at[1])

    sent(z, mate_send.at[z])
    others(ndp, d, lambda j: gt_copy(j, d).wait_send())
    others(ndp, d, lambda j: sqd_copy(j, d).wait_send())
    others(nt, t, lambda m: sqt_copy(m, t).wait_send())
    if share > 1:
        others(nt, t, lambda m: share_copy(m, t).wait_send())
    repeat(0, ndp, weigh)
    load_n.wait()

    def multiply(k):
        repeat(0, nz, lambda far: to(far * CORES + 1 - c, k, mate_send.at[far], mate).wait_recv())
        at = rows_of(k, width)
        summed = jnp.dot(wt[...], hall[k], preferred_element_type=jnp.float32)
        out_ref[:, at] = (summed + out_ref[:, at].astype(jnp.float32)).astype(jnp.bfloat16)

    def last(k):
        @pl.when(k < nk)
        def _():
            forward(nz - 2, k)
            forward(nz - 1, k)

        @pl.when(k > 0)
        def _():
            multiply(k - 1)

    repeat(0, nk + 1, last)

    def sent_on(far):
        @pl.when(far != z)
        def _():
            sent(far, mate_send.at[far])

        @pl.when((far > z) & (z > 0) & (far - z + 1 < nz - 1))
        def _():
            sent(far, fwd_send.at[far])

        @pl.when((far < z) & (z < nz - 1) & (z - far + 1 < nz - 1))
        def _():
            sent(far, fwd_send.at[far])

    repeat(0, nz, sent_on)

    @pl.when((z == 0) | (z == nz - 1))
    def _():
        sent(z, own_send.at[2])


def place(pieces, held_ref, held_norms_ref, out_ref, norms_ref, sem):
    part = out_ref.shape[0] // pieces
    copies = [pltpu.make_async_copy(held_norms_ref, norms_ref, sem.at[pieces])]
    for i in range(pieces):
        at = pl.ds(i * part, part)
        copies.append(pltpu.make_async_copy(held_ref.at[at, :], out_ref.at[at, :], sem.at[i]))
    for copy in copies:
        copy.start()
    for copy in copies:
        copy.wait()


def per_device(ndp, nt, hidden, grad_out, seg_ids, seg_counts, added_noise):
    rows, cols = added_noise.shape
    width = next(w for w in (256, 384, 128) if cols % w == 0)
    share = nt if rows % (16 * nt) == 0 else 1
    nz = ndp // CORES
    nk = cols // width
    dma = pltpu.SemaphoreType.DMA
    hbm = pl.BlockSpec(memory_space=pltpu.HBM)
    vmem = pl.BlockSpec(memory_space=pltpu.VMEM)
    out, norms = pl.pallas_call(
        functools.partial(kernel, ndp, nt, width, share),
        out_shape=(
            jax.ShapeDtypeStruct((rows, cols), jnp.bfloat16),
            jax.ShapeDtypeStruct((NSEG,), jnp.float32),
        ),
        in_specs=[hbm] * 4,
        out_specs=(vmem, vmem),
        scratch_shapes=[
            pltpu.VMEM((ndp, SEQ), jnp.int32),
            pltpu.VMEM((nk, ndp * SEQ, width), jnp.bfloat16),
            pltpu.VMEM((SEQ, D), jnp.bfloat16),
            pltpu.VMEM((D, SEQ), jnp.bfloat16),
            pltpu.VMEM((ndp, rows, SEQ), jnp.bfloat16),
            pltpu.VMEM((rows, ndp * SEQ), jnp.bfloat16),
            pltpu.VMEM((nt, NSEG, SEQ), jnp.float32),
            pltpu.VMEM((ndp, NSEG, SEQ), jnp.float32),
            dma((3,)), dma((nk,)), dma((3,)), dma((nz,)), dma((nz,)), dma((ndp, nk)), dma((ndp,)), dma((ndp,)),
            dma((nt,)), dma((nt,)), dma((nt,)), dma((nt,)), dma((ndp,)), dma((ndp,)),
        ],
        compiler_params=pltpu.CompilerParams(
            collective_id=0, has_side_effects=True, vmem_limit_bytes=32 * 1024 * 1024
        ),
        cost_estimate=pl.CostEstimate(
            flops=2 * ndp * SEQ * rows * cols, bytes_accessed=4 * rows * cols, transcendentals=0
        ),
    )(
        *(
            pltpu.with_memory_space_constraint(x, pltpu.HBM)
            for x in (seg_ids.reshape(ndp, SEQ), hidden, grad_out, added_noise)
        )
    )
    pieces = 8 if rows % 128 == 0 else 9
    return pl.pallas_call(
        functools.partial(place, pieces),
        out_shape=(
            jax.ShapeDtypeStruct((rows, cols), jnp.bfloat16),
            jax.ShapeDtypeStruct((NSEG,), jnp.float32),
        ),
        in_specs=[pl.BlockSpec(memory_space=pl.ANY)] * 2,
        out_specs=(pl.BlockSpec(memory_space=pl.ANY),) * 2,
        scratch_shapes=[dma((pieces + 1,))],
        compiler_params=pltpu.CompilerParams(vmem_limit_bytes=1024 * 1024),
        cost_estimate=pl.CostEstimate(flops=0, bytes_accessed=4 * rows * cols, transcendentals=0),
    )(out, norms)


def solution(mesh):
    placed = (P("dp", "tensor"), P("dp", None), P(), P("dp"), P("dp", "tensor"))
    return jax.shard_map(
        functools.partial(per_device, mesh.shape["dp"], mesh.shape["tensor"]),
        mesh=mesh,
        in_specs=placed,
        out_specs=(P("dp", "tensor"), P("dp")),
        check_vma=False,
    )
```

```python
import functools
import math

import jax
import jax.numpy as jnp
from jax import lax
from jax.experimental import pallas as pl
from jax.experimental.pallas import tpu as pltpu
from jax.sharding import PartitionSpec as P

D = 4608
FFW = 18432
SEQ = 128
NSEG = 8
CORES = 2

EPSILON = 1e-06
CLIP_FRACTION = 4.2
MESH = pl.DeviceIdType.MESH


def clip_bound():
    return CLIP_FRACTION * (FFW * D * NSEG / SEQ) ** 0.5


def rows_of(index, count):
    return pl.ds(pl.multiple_of(index * count, count), count)


def kernel(
    ndp, nt, width, share, ids_in, hid_ref, grad_ref, noise_ref, out_ref, norms_ref,
    ids_ref, hall, g, gt, gt_in, wt, sq_t, sq_d,
    load_sem, hid_load, own_send, fwd_send, mate_send, hid_recv, gt_send, gt_recv,
    share_send, share_recv, sqt_send, sqt_recv, sqd_send, sqd_recv, chain,
):
    d = lax.axis_index("dp")
    t = lax.axis_index("tensor")
    nz = ndp // CORES
    z = lax.div(d, CORES)
    c = lax.rem(d, CORES)
    mate = d + 1 - 2 * c
    rows, cols = out_ref.shape
    nk = cols // width
    part = rows // share

    def remote(src, dst, send, recv, device):
        return pltpu.make_async_remote_copy(
            src_ref=src, dst_ref=dst, send_sem=send, recv_sem=recv, device_id=device, device_id_type=MESH
        )

    def others(count, me, body):
        def step(i, carry):
            body(lax.rem(me + i, count))
            return carry

        lax.fori_loop(1, count, step, 0)

    def repeat(low, high, body):
        def step(i, carry):
            body(i)
            return carry

        lax.fori_loop(low, high, step, 0)

    def load_h(k):
        return pltpu.make_async_copy(
            hid_ref.at[:, rows_of(k, width)], hall.at[k, rows_of(d, SEQ), :], hid_load.at[k]
        )

    load_g = pltpu.make_async_copy(grad_ref, g, load_sem.at[0])
    load_n = pltpu.make_async_copy(noise_ref, out_ref, load_sem.at[1])
    load_i = pltpu.make_async_copy(ids_in, ids_ref, load_sem.at[2])
    repeat(0, nk, lambda k: load_h(k).start())
    load_g.start()
    load_i.start()

    def tell(sem, **device):
        pl.semaphore_signal(sem, inc=1, device_id=device, device_id_type=MESH)

    barrier = pltpu.get_barrier_semaphore()
    tell(barrier, dp=mate)

    @pl.when(z > 0)
    def _():
        tell(barrier, dp=d - CORES)

    @pl.when(z + 1 < nz)
    def _():
        tell(barrier, dp=d + CORES)

    @pl.when(z == 0)
    def _():
        others(nt, t, lambda m: tell(barrier, tensor=m))
        pl.semaphore_wait(barrier, nt + 1)

    @pl.when((z > 0) & (z + 1 < nz))
    def _():
        pl.semaphore_wait(barrier, 3)

    @pl.when(z + 1 == nz)
    def _():
        pl.semaphore_wait(barrier, 2)

    def chunk(j, k):
        return hall.at[k, rows_of(j, SEQ), :]

    def to(j, k, send, device):
        return remote(chunk(j, k), chunk(j, k), send, hid_recv.at[j, k], {"dp": device})

    def send_own(k):
        load_h(k).wait()

        @pl.when(z + 1 < nz)
        def _():
            to(d, k, own_send.at[0], d + CORES).start()

        @pl.when(z > 0)
        def _():
            to(d, k, own_send.at[1], d - CORES).start()

        to(d, k, mate_send.at[z], mate).start()

    repeat(0, nk, send_own)
    load_n.start()

    load_g.wait()

    def turn(i):
        gt[rows_of(i, SEQ), :] = g[:, rows_of(i, SEQ)].T

    repeat(0, D // SEQ, turn)
    piece = (t if share > 1 else 0) * part

    def gt_copy(j, src_seq):
        return remote(
            gt.at[pl.ds(pl.multiple_of(j * rows + piece, 16), part), :],
            gt_in.at[src_seq, pl.ds(pl.multiple_of(piece, 16), part), :],
            gt_send.at[j], gt_recv.at[src_seq], {"dp": j},
        )

    gt_in[d, pl.ds(pl.multiple_of(piece, 16), part), :] = gt[pl.ds(pl.multiple_of(d * rows + piece, 16), part), :]

    def members(j):
        ids = ids_ref[pl.ds(j, 1), :]
        inside = (lax.broadcasted_iota(jnp.int32, (NSEG, SEQ), 0) == ids).astype(jnp.float32)
        return ids, inside, jnp.sum(inside, axis=1, keepdims=True)

    load_i.wait()
    ids, inside, count = members(d)
    contract = (((1,), (1,)), ((), ()))

    def gram(k, held):
        own = hall[k, rows_of(d, SEQ), :]
        return held + lax.dot_general(own, own, contract, preferred_element_type=jnp.float32)

    gram_hidden = lax.fori_loop(0, nk, gram, jnp.zeros((SEQ, SEQ), jnp.float32))
    gram_raw = lax.dot_general(g[...], g[...], contract, preferred_element_type=jnp.float32)
    wide = jnp.broadcast_to(ids.astype(jnp.float32), (SEQ, SEQ))
    pairs = jnp.where(wide == wide.T, gram_hidden * gram_raw, 0.0)
    per_token = jnp.sum(pairs, axis=0, keepdims=True)
    partial = jnp.sum(inside * per_token, axis=1, keepdims=True)
    sq_t[t] = jnp.broadcast_to(partial, (NSEG, SEQ))

    def sqt_copy(m, src):
        return remote(sq_t.at[src], sq_t.at[src], sqt_send.at[m], sqt_recv.at[src], {"tensor": m})

    @pl.when(z + 1 < nz)
    def _():
        pl.semaphore_wait(chain.at[0], 1)

    @pl.when(z > 0)
    def _():
        tell(chain.at[0], dp=d - CORES)
        pl.semaphore_wait(chain.at[3], 1)

    @pl.when(z == 0)
    def _():
        others(nt, t, lambda m: tell(chain.at[1], tensor=m))
        pl.semaphore_wait(chain.at[1], nt - 1)
        tell(chain.at[2], dp=mate)
        pl.semaphore_wait(chain.at[2], 1)

    @pl.when(z + 1 < nz)
    def _():
        tell(chain.at[3], dp=d + CORES)

    others(nt, t, lambda m: sqt_copy(m, t).start())
    others(ndp, d, lambda j: gt_copy(j, d).start())
    others(nt, t, lambda m: sqt_copy(m, m).wait_recv())
    total = sq_t[0]
    for m in range(1, nt):
        total = total + sq_t[m]
    total = total / (count * count)
    sq_d[d] = total
    norms_ref[...] = jnp.sqrt(total + EPSILON)[:, 0]

    def sqd_copy(j, src):
        return remote(sq_d.at[src], sq_d.at[src], sqd_send.at[j], sqd_recv.at[src], {"dp": j})

    others(ndp, d, lambda j: sqd_copy(j, d).start())

    def forward(h, k):
        for way in (1, -1):
            far = z + way * h
            ahead = z - way

            @pl.when((far >= 0) & (far < nz))
            def _():
                j = far * CORES + c
                to(j, k, mate_send.at[far], mate).wait_recv()

                @pl.when((ahead >= 0) & (ahead < nz))
                def _():
                    to(j, k, fwd_send.at[far], ahead * CORES + c).start()

                to(j, k, mate_send.at[far], mate).start()

    repeat(0, nk, lambda k: forward(1, k))

    others(ndp, d, lambda j: gt_copy(j, j).wait_recv())

    def share_copy(m, src):
        block = gt_in.at[:, pl.ds(pl.multiple_of(src * part, 16), part), :]
        return remote(block, block, share_send.at[m], share_recv.at[src], {"tensor": m})

    if share > 1:
        others(nt, t, lambda m: share_copy(m, t).start())
    repeat(nk, nk * (nz - 2), lambda i: forward(1 + lax.div(i, nk), lax.rem(i, nk)))
    if share > 1:
        others(nt, t, lambda m: share_copy(m, m).wait_recv())
    others(ndp, d, lambda j: sqd_copy(j, j).wait_recv())

    def weigh(j):
        _, inside, count = members(j)
        norm = jnp.sqrt(sq_d[j] + EPSILON)
        factor = jnp.minimum(1.0, clip_bound() / norm)
        tok_count = jnp.sum(inside * count, axis=0, keepdims=True)
        tok_factor = jnp.sum(inside * factor, axis=0, keepdims=True)
        scaled = (gt_in[j].astype(jnp.float32) / tok_count).astype(jnp.bfloat16)
        wt[:, rows_of(j, SEQ)] = (scaled.astype(jnp.float32) * tok_factor).astype(jnp.bfloat16)

    def sent(far, sem):
        block = hall.at[:, rows_of(far * CORES + c, SEQ), :]
        remote(block, block, sem, hid_recv.at[0, 0], {"dp": mate}).wait_send()

    @pl.when(z + 1 < nz)
    def _():
        sent(z, own_send.at[0])

    @pl.when(z > 0)
    def _():
        sent(z, own_send.at[1])

    sent(z, mate_send.at[z])
    others(ndp, d, lambda j: gt_copy(j, d).wait_send())
    others(ndp, d, lambda j: sqd_copy(j, d).wait_send())
    others(nt, t, lambda m: sqt_copy(m, t).wait_send())
    if share > 1:
        others(nt, t, lambda m: share_copy(m, t).wait_send())
    repeat(0, ndp, weigh)
    load_n.wait()

    def multiply(k):
        repeat(0, nz, lambda far: to(far * CORES + 1 - c, k, mate_send.at[far], mate).wait_recv())
        at = rows_of(k, width)
        summed = jnp.dot(wt[...], hall[k], preferred_element_type=jnp.float32)
        out_ref[:, at] = (summed + out_ref[:, at].astype(jnp.float32)).astype(jnp.bfloat16)

    def last(k):
        @pl.when(k < nk)
        def _():
            forward(nz - 1, k)

        @pl.when(k > 0)
        def _():
            multiply(k - 1)

    repeat(0, nk + 1, last)

    def sent_on(far):
        @pl.when(far != z)
        def _():
            sent(far, mate_send.at[far])

        @pl.when((z > 0) & (z < nz - 1) & (far != z))
        def _():
            sent(far, fwd_send.at[far])

    repeat(0, nz, sent_on)


def place(pieces, held_ref, held_norms_ref, out_ref, norms_ref, sem):
    part = out_ref.shape[0] // pieces
    copies = [pltpu.make_async_copy(held_norms_ref, norms_ref, sem.at[pieces])]
    for i in range(pieces):
        at = pl.ds(i * part, part)
        copies.append(pltpu.make_async_copy(held_ref.at[at, :], out_ref.at[at, :], sem.at[i]))
    for copy in copies:
        copy.start()
    for copy in copies:
        copy.wait()


def per_device(ndp, nt, hidden, grad_out, seg_ids, seg_counts, added_noise):
    rows, cols = added_noise.shape
    width = next(w for w in (256, 384, 128) if cols % w == 0)
    share = nt if rows % (16 * nt) == 0 else 1
    nz = ndp // CORES
    nk = cols // width
    dma = pltpu.SemaphoreType.DMA
    hbm = pl.BlockSpec(memory_space=pltpu.HBM)
    vmem = pl.BlockSpec(memory_space=pltpu.VMEM)
    out, norms = pl.pallas_call(
        functools.partial(kernel, ndp, nt, width, share),
        out_shape=(
            jax.ShapeDtypeStruct((rows, cols), jnp.bfloat16),
            jax.ShapeDtypeStruct((NSEG,), jnp.float32),
        ),
        in_specs=[hbm] * 4,
        out_specs=(vmem, vmem),
        scratch_shapes=[
            pltpu.VMEM((ndp, SEQ), jnp.int32),
            pltpu.VMEM((nk, ndp * SEQ, width), jnp.bfloat16),
            pltpu.VMEM((SEQ, D), jnp.bfloat16),
            pltpu.VMEM((D, SEQ), jnp.bfloat16),
            pltpu.VMEM((ndp, rows, SEQ), jnp.bfloat16),
            pltpu.VMEM((rows, ndp * SEQ), jnp.bfloat16),
            pltpu.VMEM((nt, NSEG, SEQ), jnp.float32),
            pltpu.VMEM((ndp, NSEG, SEQ), jnp.float32),
            dma((3,)), dma((nk,)), dma((2,)), dma((nz,)), dma((nz,)), dma((ndp, nk)), dma((ndp,)), dma((ndp,)),
            dma((nt,)), dma((nt,)), dma((nt,)), dma((nt,)), dma((ndp,)), dma((ndp,)),
            pltpu.SemaphoreType.REGULAR((4,)),
        ],
        compiler_params=pltpu.CompilerParams(
            collective_id=0, has_side_effects=True, vmem_limit_bytes=32 * 1024 * 1024
        ),
        cost_estimate=pl.CostEstimate(
            flops=2 * ndp * SEQ * rows * cols, bytes_accessed=4 * rows * cols, transcendentals=0
        ),
    )(
        *(
            pltpu.with_memory_space_constraint(x, pltpu.HBM)
            for x in (seg_ids.reshape(ndp, SEQ), hidden, grad_out, added_noise)
        )
    )
    pieces = 8 if rows % 128 == 0 else 9
    return pl.pallas_call(
        functools.partial(place, pieces),
        out_shape=(
            jax.ShapeDtypeStruct((rows, cols), jnp.bfloat16),
            jax.ShapeDtypeStruct((NSEG,), jnp.float32),
        ),
        in_specs=[pl.BlockSpec(memory_space=pl.ANY)] * 2,
        out_specs=(pl.BlockSpec(memory_space=pl.ANY),) * 2,
        scratch_shapes=[dma((pieces + 1,))],
        compiler_params=pltpu.CompilerParams(vmem_limit_bytes=1024 * 1024),
        cost_estimate=pl.CostEstimate(flops=0, bytes_accessed=4 * rows * cols, transcendentals=0),
    )(out, norms)


def solution(mesh):
    placed = (P("dp", "tensor"), P("dp", None), P(), P("dp"), P("dp", "tensor"))
    return jax.shard_map(
        functools.partial(per_device, mesh.shape["dp"], mesh.shape["tensor"]),
        mesh=mesh,
        in_specs=placed,
        out_specs=(P("dp", "tensor"), P("dp")),
        check_vma=False,
    )
```

```python
import functools
import math

import jax
import jax.numpy as jnp
from jax import lax
from jax.experimental import pallas as pl
from jax.experimental.pallas import tpu as pltpu
from jax.sharding import PartitionSpec as P

D = 4608
FFW = 18432
SEQ = 128
NSEG = 8
CORES = 2

EPSILON = 1e-06
CLIP_FRACTION = 4.2
MESH = pl.DeviceIdType.MESH


def clip_bound():
    return CLIP_FRACTION * (FFW * D * NSEG / SEQ) ** 0.5


def rows_of(index, count):
    return pl.ds(pl.multiple_of(index * count, count), count)


def kernel(
    ndp, nt, share, keep, ids_in, hid_ref, grad_ref, noise_ref, out_ref, norms_ref, hall, wt,
    ids_ref, g, gt, gt_in, sq_t, sq_d,
    load_sem, hid_load, own_send, fwd_send, mate_send, hid_recv, gt_send, gt_recv,
    share_send, share_recv, sqt_send, sqt_recv, sqd_send, sqd_recv, chain,
):
    d = lax.axis_index("dp")
    t = lax.axis_index("tensor")
    nz = ndp // CORES
    z = lax.div(d, CORES)
    c = lax.rem(d, CORES)
    mate = d + 1 - 2 * c
    rows, cols = out_ref.shape
    nk, _, width = hall.shape
    part = rows // share

    def remote(src, dst, send, recv, device):
        return pltpu.make_async_remote_copy(
            src_ref=src, dst_ref=dst, send_sem=send, recv_sem=recv, device_id=device, device_id_type=MESH
        )

    def others(count, me, body):
        def step(i, carry):
            body(lax.rem(me + i, count))
            return carry

        lax.fori_loop(1, count, step, 0)

    def repeat(low, high, body):
        def step(i, carry):
            body(i)
            return carry

        lax.fori_loop(low, high, step, 0)

    def load_h(k):
        return pltpu.make_async_copy(
            hid_ref.at[:, rows_of(k, width)], hall.at[k, rows_of(d, SEQ), :], hid_load.at[k]
        )

    load_g = pltpu.make_async_copy(grad_ref, g, load_sem.at[0])
    load_n = pltpu.make_async_copy(noise_ref, out_ref, load_sem.at[1])
    load_i = pltpu.make_async_copy(ids_in, ids_ref, load_sem.at[2])
    repeat(0, nk, lambda k: load_h(k).start())
    load_g.start()
    load_i.start()

    def tell(sem, **device):
        pl.semaphore_signal(sem, inc=1, device_id=device, device_id_type=MESH)

    barrier = pltpu.get_barrier_semaphore()
    tell(barrier, dp=mate)

    @pl.when(z > 0)
    def _():
        tell(barrier, dp=d - CORES)

    @pl.when(z + 1 < nz)
    def _():
        tell(barrier, dp=d + CORES)

    @pl.when(z == 0)
    def _():
        others(nt, t, lambda m: tell(barrier, tensor=m))
        pl.semaphore_wait(barrier, nt + 1)

    @pl.when((z > 0) & (z + 1 < nz))
    def _():
        pl.semaphore_wait(barrier, 3)

    @pl.when(z + 1 == nz)
    def _():
        pl.semaphore_wait(barrier, 2)

    def chunk(j, k):
        return hall.at[k, rows_of(j, SEQ), :]

    def to(j, k, send, device):
        return remote(chunk(j, k), chunk(j, k), send, hid_recv.at[j, k], {"dp": device})

    def send_own(k):
        load_h(k).wait()

        @pl.when(z + 1 < nz)
        def _():
            to(d, k, own_send.at[0], d + CORES).start()

        @pl.when(z > 0)
        def _():
            to(d, k, own_send.at[1], d - CORES).start()

        to(d, k, mate_send.at[z], mate).start()

    repeat(0, nk, send_own)
    load_n.start()

    load_g.wait()

    def turn(i):
        gt[rows_of(i, SEQ), :] = g[:, rows_of(i, SEQ)].T

    repeat(0, D // SEQ, turn)
    piece = (t if share > 1 else 0) * part

    def gt_copy(j, src_seq):
        return remote(
            gt.at[pl.ds(pl.multiple_of(j * rows + piece, 16), part), :],
            gt_in.at[src_seq, pl.ds(pl.multiple_of(piece, 16), part), :],
            gt_send.at[j], gt_recv.at[src_seq], {"dp": j},
        )

    gt_in[d, pl.ds(pl.multiple_of(piece, 16), part), :] = gt[pl.ds(pl.multiple_of(d * rows + piece, 16), part), :]

    def members(j):
        ids = ids_ref[pl.ds(j, 1), :]
        inside = (lax.broadcasted_iota(jnp.int32, (NSEG, SEQ), 0) == ids).astype(jnp.float32)
        return ids, inside, jnp.sum(inside, axis=1, keepdims=True)

    load_i.wait()
    ids, inside, count = members(d)
    contract = (((1,), (1,)), ((), ()))

    def gram(k, held):
        own = hall[k, rows_of(d, SEQ), :]
        return held + lax.dot_general(own, own, contract, preferred_element_type=jnp.float32)

    gram_hidden = lax.fori_loop(0, nk, gram, jnp.zeros((SEQ, SEQ), jnp.float32))
    gram_raw = lax.dot_general(g[...], g[...], contract, preferred_element_type=jnp.float32)
    wide = jnp.broadcast_to(ids.astype(jnp.float32), (SEQ, SEQ))
    pairs = jnp.where(wide == wide.T, gram_hidden * gram_raw, 0.0)
    per_token = jnp.sum(pairs, axis=0, keepdims=True)
    partial = jnp.sum(inside * per_token, axis=1, keepdims=True)
    sq_t[t] = jnp.broadcast_to(partial, (NSEG, SEQ))

    def sqt_copy(m, src):
        return remote(sq_t.at[src], sq_t.at[src], sqt_send.at[m], sqt_recv.at[src], {"tensor": m})

    @pl.when(z + 1 < nz)
    def _():
        pl.semaphore_wait(chain.at[0], 1)

    @pl.when(z > 0)
    def _():
        tell(chain.at[0], dp=d - CORES)
        pl.semaphore_wait(chain.at[3], 1)

    @pl.when(z == 0)
    def _():
        others(nt, t, lambda m: tell(chain.at[1], tensor=m))
        pl.semaphore_wait(chain.at[1], nt - 1)
        tell(chain.at[2], dp=mate)
        pl.semaphore_wait(chain.at[2], 1)

    @pl.when(z + 1 < nz)
    def _():
        tell(chain.at[3], dp=d + CORES)

    others(nt, t, lambda m: sqt_copy(m, t).start())
    others(ndp, d, lambda j: gt_copy(j, d).start())
    others(nt, t, lambda m: sqt_copy(m, m).wait_recv())
    total = sq_t[0]
    for m in range(1, nt):
        total = total + sq_t[m]
    total = total / (count * count)
    sq_d[d] = total
    norms_ref[...] = jnp.sqrt(total + EPSILON)[:, 0]

    def sqd_copy(j, src):
        return remote(sq_d.at[src], sq_d.at[src], sqd_send.at[j], sqd_recv.at[src], {"dp": j})

    others(ndp, d, lambda j: sqd_copy(j, d).start())

    def forward(h, k):
        for way in (1, -1):
            far = z + way * h
            ahead = z - way

            @pl.when((far >= 0) & (far < nz))
            def _():
                j = far * CORES + c
                to(j, k, mate_send.at[far], mate).wait_recv()

                @pl.when((ahead >= 0) & (ahead < nz))
                def _():
                    to(j, k, fwd_send.at[far], ahead * CORES + c).start()

                to(j, k, mate_send.at[far], mate).start()

    repeat(0, nk, lambda k: forward(1, k))

    others(ndp, d, lambda j: gt_copy(j, j).wait_recv())

    def share_copy(m, src):
        block = gt_in.at[:, pl.ds(pl.multiple_of(src * part, 16), part), :]
        return remote(block, block, share_send.at[m], share_recv.at[src], {"tensor": m})

    if share > 1:
        others(nt, t, lambda m: share_copy(m, t).start())
    repeat(nk, nk * (nz - 2), lambda i: forward(1 + lax.div(i, nk), lax.rem(i, nk)))
    if share > 1:
        others(nt, t, lambda m: share_copy(m, m).wait_recv())
    others(ndp, d, lambda j: sqd_copy(j, j).wait_recv())

    def weigh(j):
        _, inside, count = members(j)
        norm = jnp.sqrt(sq_d[j] + EPSILON)
        factor = jnp.minimum(1.0, clip_bound() / norm)
        tok_count = jnp.sum(inside * count, axis=0, keepdims=True)
        tok_factor = jnp.sum(inside * factor, axis=0, keepdims=True)
        scaled = (gt_in[j].astype(jnp.float32) / tok_count).astype(jnp.bfloat16)
        wt[:, rows_of(j, SEQ)] = (scaled.astype(jnp.float32) * tok_factor).astype(jnp.bfloat16)

    def sent(far, sem):
        block = hall.at[:, rows_of(far * CORES + c, SEQ), :]
        remote(block, block, sem, hid_recv.at[0, 0], {"dp": mate}).wait_send()

    @pl.when(z + 1 < nz)
    def _():
        sent(z, own_send.at[0])

    @pl.when(z > 0)
    def _():
        sent(z, own_send.at[1])

    sent(z, mate_send.at[z])
    others(ndp, d, lambda j: gt_copy(j, d).wait_send())
    others(ndp, d, lambda j: sqd_copy(j, d).wait_send())
    others(nt, t, lambda m: sqt_copy(m, t).wait_send())
    if share > 1:
        others(nt, t, lambda m: share_copy(m, t).wait_send())
    repeat(0, ndp, weigh)
    load_n.wait()

    def multiply(k):
        repeat(0, nz, lambda far: to(far * CORES + 1 - c, k, mate_send.at[far], mate).wait_recv())

        @pl.when(k < nk - keep)
        def _():
            at = rows_of(k, width)
            summed = jnp.dot(wt[...], hall[k], preferred_element_type=jnp.float32)
            out_ref[:, at] = (summed + out_ref[:, at].astype(jnp.float32)).astype(jnp.bfloat16)

    def last(k):
        @pl.when(k < nk)
        def _():
            forward(nz - 1, k)

        @pl.when(k > 0)
        def _():
            multiply(k - 1)

    repeat(0, nk + 1, last)

    def sent_on(far):
        @pl.when(far != z)
        def _():
            sent(far, mate_send.at[far])

        @pl.when((z > 0) & (z < nz - 1) & (far != z))
        def _():
            sent(far, fwd_send.at[far])

    repeat(0, nz, sent_on)


def place(keep, pieces, held_ref, held_norms_ref, hall, wt, out_ref, norms_ref, done, sem):
    rows = out_ref.shape[0]
    nk, _, width = hall.shape
    part = rows // pieces
    ready = (nk - keep) * width
    copies = []

    def put(src, dst):
        copies.append(pltpu.make_async_copy(src, dst, sem.at[len(copies)]))
        copies[-1].start()

    for i in range(pieces):
        at = (pl.ds(i * part, part), pl.ds(0, ready))
        put(held_ref.at[at], out_ref.at[at])
    put(held_norms_ref, norms_ref)
    for i in range(keep):
        at = pl.ds(ready + i * width, width)
        summed = jnp.dot(wt[...], hall[nk - keep + i], preferred_element_type=jnp.float32)
        done[i] = (summed + held_ref[:, at].astype(jnp.float32)).astype(jnp.bfloat16)
        put(done.at[i], out_ref.at[:, at])
    for copy in copies:
        copy.wait()


def per_device(ndp, nt, hidden, grad_out, seg_ids, seg_counts, added_noise):
    rows, cols = added_noise.shape
    width = next(w for w in (256, 384, 128) if cols % w == 0)
    share = nt if rows % (16 * nt) == 0 else 1
    nz = ndp // CORES
    nk = cols // width
    dma = pltpu.SemaphoreType.DMA
    hbm = pl.BlockSpec(memory_space=pltpu.HBM)
    vmem = pl.BlockSpec(memory_space=pltpu.VMEM)
    keep = min(3, nk // 2)
    out, norms, hall, wt = pl.pallas_call(
        functools.partial(kernel, ndp, nt, share, keep),
        out_shape=(
            jax.ShapeDtypeStruct((rows, cols), jnp.bfloat16),
            jax.ShapeDtypeStruct((NSEG,), jnp.float32),
            pltpu.VMEM((nk, ndp * SEQ, width), jnp.bfloat16),
            pltpu.VMEM((rows, ndp * SEQ), jnp.bfloat16),
        ),
        in_specs=[hbm] * 4,
        out_specs=(vmem,) * 4,
        scratch_shapes=[
            pltpu.VMEM((ndp, SEQ), jnp.int32),
            pltpu.VMEM((SEQ, D), jnp.bfloat16),
            pltpu.VMEM((D, SEQ), jnp.bfloat16),
            pltpu.VMEM((ndp, rows, SEQ), jnp.bfloat16),
            pltpu.VMEM((nt, NSEG, SEQ), jnp.float32),
            pltpu.VMEM((ndp, NSEG, SEQ), jnp.float32),
            dma((3,)), dma((nk,)), dma((2,)), dma((nz,)), dma((nz,)), dma((ndp, nk)), dma((ndp,)), dma((ndp,)),
            dma((nt,)), dma((nt,)), dma((nt,)), dma((nt,)), dma((ndp,)), dma((ndp,)),
            pltpu.SemaphoreType.REGULAR((4,)),
        ],
        compiler_params=pltpu.CompilerParams(
            collective_id=0, has_side_effects=True, vmem_limit_bytes=24 * 1024 * 1024
        ),
        cost_estimate=pl.CostEstimate(
            flops=2 * ndp * SEQ * rows * cols, bytes_accessed=4 * rows * cols, transcendentals=0
        ),
    )(
        *(
            pltpu.with_memory_space_constraint(x, pltpu.HBM)
            for x in (seg_ids.reshape(ndp, SEQ), hidden, grad_out, added_noise)
        )
    )
    pieces = 8 if rows % 128 == 0 else 9
    return pl.pallas_call(
        functools.partial(place, keep, pieces),
        out_shape=(
            jax.ShapeDtypeStruct((rows, cols), jnp.bfloat16),
            jax.ShapeDtypeStruct((NSEG,), jnp.float32),
        ),
        in_specs=[vmem] * 4,
        out_specs=(pl.BlockSpec(memory_space=pl.ANY),) * 2,
        scratch_shapes=[pltpu.VMEM((keep, rows, width), jnp.bfloat16), dma((pieces + 1 + keep,))],
        compiler_params=pltpu.CompilerParams(vmem_limit_bytes=8 * 1024 * 1024),
        cost_estimate=pl.CostEstimate(flops=2 * ndp * SEQ * rows * width * keep, bytes_accessed=4 * rows * cols, transcendentals=0),
    )(out, norms, hall, wt)


def solution(mesh):
    placed = (P("dp", "tensor"), P("dp", None), P(), P("dp"), P("dp", "tensor"))
    return jax.shard_map(
        functools.partial(per_device, mesh.shape["dp"], mesh.shape["tensor"]),
        mesh=mesh,
        in_specs=placed,
        out_specs=(P("dp", "tensor"), P("dp")),
        check_vma=False,
    )
```

```python
import functools
import math

import jax
import jax.numpy as jnp
from jax import lax
from jax.experimental import pallas as pl
from jax.experimental.pallas import tpu as pltpu
from jax.sharding import PartitionSpec as P

D = 4608
FFW = 18432
SEQ = 128
NSEG = 8
CORES = 2

EPSILON = 1e-06
CLIP_FRACTION = 4.2
MESH = pl.DeviceIdType.MESH


def clip_bound():
    return CLIP_FRACTION * (FFW * D * NSEG / SEQ) ** 0.5


def rows_of(index, count):
    return pl.ds(pl.multiple_of(index * count, count), count)


def kernel(
    ndp, nt, width, share, ids_in, hid_ref, grad_ref, noise_ref, out_ref, norms_ref,
    ids_ref, hall, g, gt, gt_in, wt, sq_t, sq_d,
    load_sem, hid_load, own_send, fwd_send, mate_send, hid_recv, gt_send, gt_recv,
    share_send, share_recv, sqt_send, sqt_recv, sqd_send, sqd_recv, chain,
):
    d = lax.axis_index("dp")
    t = lax.axis_index("tensor")
    nz = ndp // CORES
    z = lax.div(d, CORES)
    c = lax.rem(d, CORES)
    mate = d + 1 - 2 * c
    rows, cols = out_ref.shape
    nk = cols // width
    part = rows // share

    def remote(src, dst, send, recv, device):
        return pltpu.make_async_remote_copy(
            src_ref=src, dst_ref=dst, send_sem=send, recv_sem=recv, device_id=device, device_id_type=MESH
        )

    def others(count, me, body):
        def step(i, carry):
            body(lax.rem(me + i, count))
            return carry

        lax.fori_loop(1, count, step, 0)

    def repeat(low, high, body):
        def step(i, carry):
            body(i)
            return carry

        lax.fori_loop(low, high, step, 0)

    def load_h(k):
        return pltpu.make_async_copy(
            hid_ref.at[:, rows_of(k, width)], hall.at[k, rows_of(d, SEQ), :], hid_load.at[k]
        )

    load_g = pltpu.make_async_copy(grad_ref, g, load_sem.at[0])
    load_n = pltpu.make_async_copy(noise_ref, out_ref, load_sem.at[1])
    load_i = pltpu.make_async_copy(ids_in, ids_ref, load_sem.at[2])
    repeat(0, nk, lambda k: load_h(k).start())
    load_g.start()
    load_i.start()

    def tell(sem, **device):
        pl.semaphore_signal(sem, inc=1, device_id=device, device_id_type=MESH)

    barrier = pltpu.get_barrier_semaphore()
    tell(barrier, dp=mate)

    @pl.when(z + 1 < nz)
    def _():
        tell(barrier, dp=d + CORES)

    @pl.when(z == 0)
    def _():
        others(nt, t, lambda m: tell(barrier, tensor=m))
        pl.semaphore_wait(barrier, nt)

    @pl.when(z > 0)
    def _():
        pl.semaphore_wait(barrier, 2)
        tell(chain.at[4], dp=d - CORES)

    def chunk(j, k):
        return hall.at[k, rows_of(j, SEQ), :]

    def to(j, k, send, device):
        return remote(chunk(j, k), chunk(j, k), send, hid_recv.at[j, k], {"dp": device})

    def send_down(k):
        load_h(k).wait()

        @pl.when(z > 0)
        def _():
            to(d, k, own_send.at[1], d - CORES).start()

        to(d, k, mate_send.at[z], mate).start()

    def send_up(k):
        @pl.when(z + 1 < nz)
        def _():
            to(d, k, own_send.at[0], d + CORES).start()

    def send_both(k):
        send_down(k)
        send_up(k)

    early = min(4, nk)
    repeat(0, early, send_down)

    @pl.when(z + 1 < nz)
    def _():
        pl.semaphore_wait(chain.at[4], 1)

    repeat(0, early, send_up)
    repeat(early, nk, send_both)
    load_n.start()

    load_g.wait()

    def turn(i):
        gt[rows_of(i, SEQ), :] = g[:, rows_of(i, SEQ)].T

    repeat(0, D // SEQ, turn)
    piece = (t if share > 1 else 0) * part

    def gt_copy(j, src_seq):
        return remote(
            gt.at[pl.ds(pl.multiple_of(j * rows + piece, 16), part), :],
            gt_in.at[src_seq, pl.ds(pl.multiple_of(piece, 16), part), :],
            gt_send.at[j], gt_recv.at[src_seq], {"dp": j},
        )

    gt_in[d, pl.ds(pl.multiple_of(piece, 16), part), :] = gt[pl.ds(pl.multiple_of(d * rows + piece, 16), part), :]

    def members(j):
        ids = ids_ref[pl.ds(j, 1), :]
        inside = (lax.broadcasted_iota(jnp.int32, (NSEG, SEQ), 0) == ids).astype(jnp.float32)
        return ids, inside, jnp.sum(inside, axis=1, keepdims=True)

    load_i.wait()
    ids, inside, count = members(d)
    contract = (((1,), (1,)), ((), ()))

    def gram(k, held):
        own = hall[k, rows_of(d, SEQ), :]
        return held + lax.dot_general(own, own, contract, preferred_element_type=jnp.float32)

    gram_hidden = lax.fori_loop(0, nk, gram, jnp.zeros((SEQ, SEQ), jnp.float32))
    gram_raw = lax.dot_general(g[...], g[...], contract, preferred_element_type=jnp.float32)
    wide = jnp.broadcast_to(ids.astype(jnp.float32), (SEQ, SEQ))
    pairs = jnp.where(wide == wide.T, gram_hidden * gram_raw, 0.0)
    per_token = jnp.sum(pairs, axis=0, keepdims=True)
    partial = jnp.sum(inside * per_token, axis=1, keepdims=True)
    sq_t[t] = jnp.broadcast_to(partial, (NSEG, SEQ))

    def sqt_copy(m, src):
        return remote(sq_t.at[src], sq_t.at[src], sqt_send.at[m], sqt_recv.at[src], {"tensor": m})

    @pl.when(z + 1 < nz)
    def _():
        pl.semaphore_wait(chain.at[0], 1)

    @pl.when(z > 0)
    def _():
        tell(chain.at[0], dp=d - CORES)
        pl.semaphore_wait(chain.at[3], 1)

    @pl.when(z == 0)
    def _():
        others(nt, t, lambda m: tell(chain.at[1], tensor=m))
        pl.semaphore_wait(chain.at[1], nt - 1)
        tell(chain.at[2], dp=mate)
        pl.semaphore_wait(chain.at[2], 1)

    @pl.when(z + 1 < nz)
    def _():
        tell(chain.at[3], dp=d + CORES)

    others(nt, t, lambda m: sqt_copy(m, t).start())
    others(ndp, d, lambda j: gt_copy(j, d).start())
    others(nt, t, lambda m: sqt_copy(m, m).wait_recv())
    total = sq_t[0]
    for m in range(1, nt):
        total = total + sq_t[m]
    total = total / (count * count)
    sq_d[d] = total
    norms_ref[...] = jnp.sqrt(total + EPSILON)[:, 0]

    def sqd_copy(j, src):
        return remote(sq_d.at[src], sq_d.at[src], sqd_send.at[j], sqd_recv.at[src], {"dp": j})

    others(ndp, d, lambda j: sqd_copy(j, d).start())

    def forward(h, k):
        for way in (1, -1):
            far = z + way * h
            ahead = z - way

            @pl.when((far >= 0) & (far < nz))
            def _():
                j = far * CORES + c
                to(j, k, mate_send.at[far], mate).wait_recv()

                @pl.when((ahead >= 0) & (ahead < nz))
                def _():
                    to(j, k, fwd_send.at[far], ahead * CORES + c).start()

                to(j, k, mate_send.at[far], mate).start()

    repeat(0, nk, lambda k: forward(1, k))

    others(ndp, d, lambda j: gt_copy(j, j).wait_recv())

    def share_copy(m, src):
        block = gt_in.at[:, pl.ds(pl.multiple_of(src * part, 16), part), :]
        return remote(block, block, share_send.at[m], share_recv.at[src], {"tensor": m})

    if share > 1:
        others(nt, t, lambda m: share_copy(m, t).start())
    repeat(nk, nk * (nz - 2), lambda i: forward(1 + lax.div(i, nk), lax.rem(i, nk)))
    if share > 1:
        others(nt, t, lambda m: share_copy(m, m).wait_recv())
    others(ndp, d, lambda j: sqd_copy(j, j).wait_recv())

    def weigh(j):
        _, inside, count = members(j)
        norm = jnp.sqrt(sq_d[j] + EPSILON)
        factor = jnp.minimum(1.0, clip_bound() / norm)
        tok_count = jnp.sum(inside * count, axis=0, keepdims=True)
        tok_factor = jnp.sum(inside * factor, axis=0, keepdims=True)
        scaled = (gt_in[j].astype(jnp.float32) / tok_count).astype(jnp.bfloat16)
        wt[:, rows_of(j, SEQ)] = (scaled.astype(jnp.float32) * tok_factor).astype(jnp.bfloat16)

    def sent(far, sem):
        block = hall.at[:, rows_of(far * CORES + c, SEQ), :]
        remote(block, block, sem, hid_recv.at[0, 0], {"dp": mate}).wait_send()

    @pl.when(z + 1 < nz)
    def _():
        sent(z, own_send.at[0])

    @pl.when(z > 0)
    def _():
        sent(z, own_send.at[1])

    sent(z, mate_send.at[z])
    others(ndp, d, lambda j: gt_copy(j, d).wait_send())
    others(ndp, d, lambda j: sqd_copy(j, d).wait_send())
    others(nt, t, lambda m: sqt_copy(m, t).wait_send())
    if share > 1:
        others(nt, t, lambda m: share_copy(m, t).wait_send())
    repeat(0, ndp, weigh)
    load_n.wait()

    def multiply(k):
        repeat(0, nz, lambda far: to(far * CORES + 1 - c, k, mate_send.at[far], mate).wait_recv())
        at = rows_of(k, width)
        summed = jnp.dot(wt[...], hall[k], preferred_element_type=jnp.float32)
        out_ref[:, at] = (summed + out_ref[:, at].astype(jnp.float32)).astype(jnp.bfloat16)

    def last(k):
        @pl.when(k < nk)
        def _():
            forward(nz - 1, k)

        @pl.when(k > 0)
        def _():
            multiply(k - 1)

    repeat(0, nk + 1, last)

    def sent_on(far):
        @pl.when(far != z)
        def _():
            sent(far, mate_send.at[far])

        @pl.when((z > 0) & (z < nz - 1) & (far != z))
        def _():
            sent(far, fwd_send.at[far])

    repeat(0, nz, sent_on)


def place(pieces, held_ref, held_norms_ref, out_ref, norms_ref, sem):
    part = out_ref.shape[0] // pieces
    copies = [pltpu.make_async_copy(held_norms_ref, norms_ref, sem.at[pieces])]
    for i in range(pieces):
        at = pl.ds(i * part, part)
        copies.append(pltpu.make_async_copy(held_ref.at[at, :], out_ref.at[at, :], sem.at[i]))
    for i, copy in enumerate(copies):
        copy.start(priority=i % 2)
    for copy in copies:
        copy.wait()


def per_device(ndp, nt, hidden, grad_out, seg_ids, seg_counts, added_noise):
    rows, cols = added_noise.shape
    width = next(w for w in (256, 384, 128) if cols % w == 0)
    share = nt if rows % (16 * nt) == 0 else 1
    nz = ndp // CORES
    nk = cols // width
    dma = pltpu.SemaphoreType.DMA
    hbm = pl.BlockSpec(memory_space=pltpu.HBM)
    vmem = pl.BlockSpec(memory_space=pltpu.VMEM)
    out, norms = pl.pallas_call(
        functools.partial(kernel, ndp, nt, width, share),
        out_shape=(
            jax.ShapeDtypeStruct((rows, cols), jnp.bfloat16),
            jax.ShapeDtypeStruct((NSEG,), jnp.float32),
        ),
        in_specs=[hbm] * 4,
        out_specs=(vmem, vmem),
        scratch_shapes=[
            pltpu.VMEM((ndp, SEQ), jnp.int32),
            pltpu.VMEM((nk, ndp * SEQ, width), jnp.bfloat16),
            pltpu.VMEM((SEQ, D), jnp.bfloat16),
            pltpu.VMEM((D, SEQ), jnp.bfloat16),
            pltpu.VMEM((ndp, rows, SEQ), jnp.bfloat16),
            pltpu.VMEM((rows, ndp * SEQ), jnp.bfloat16),
            pltpu.VMEM((nt, NSEG, SEQ), jnp.float32),
            pltpu.VMEM((ndp, NSEG, SEQ), jnp.float32),
            dma((3,)), dma((nk,)), dma((2,)), dma((nz,)), dma((nz,)), dma((ndp, nk)), dma((ndp,)), dma((ndp,)),
            dma((nt,)), dma((nt,)), dma((nt,)), dma((nt,)), dma((ndp,)), dma((ndp,)),
            pltpu.SemaphoreType.REGULAR((5,)),
        ],
        compiler_params=pltpu.CompilerParams(
            collective_id=0, has_side_effects=True, vmem_limit_bytes=32 * 1024 * 1024
        ),
        cost_estimate=pl.CostEstimate(
            flops=2 * ndp * SEQ * rows * cols, bytes_accessed=4 * rows * cols, transcendentals=0
        ),
    )(
        *(
            pltpu.with_memory_space_constraint(x, pltpu.HBM)
            for x in (seg_ids.reshape(ndp, SEQ), hidden, grad_out, added_noise)
        )
    )
    pieces = 8 if rows % 128 == 0 else 9
    return pl.pallas_call(
        functools.partial(place, pieces),
        out_shape=(
            jax.ShapeDtypeStruct((rows, cols), jnp.bfloat16),
            jax.ShapeDtypeStruct((NSEG,), jnp.float32),
        ),
        in_specs=[pl.BlockSpec(memory_space=pl.ANY)] * 2,
        out_specs=(pl.BlockSpec(memory_space=pl.ANY),) * 2,
        scratch_shapes=[dma((pieces + 1,))],
        compiler_params=pltpu.CompilerParams(vmem_limit_bytes=1024 * 1024),
        cost_estimate=pl.CostEstimate(flops=0, bytes_accessed=4 * rows * cols, transcendentals=0),
    )(out, norms)


def solution(mesh):
    placed = (P("dp", "tensor"), P("dp", None), P(), P("dp"), P("dp", "tensor"))
    return jax.shard_map(
        functools.partial(per_device, mesh.shape["dp"], mesh.shape["tensor"]),
        mesh=mesh,
        in_specs=placed,
        out_specs=(P("dp", "tensor"), P("dp")),
        check_vma=False,
    )
```

```python
import functools
import math

import jax
import jax.numpy as jnp
from jax import lax
from jax.experimental import pallas as pl
from jax.experimental.pallas import tpu as pltpu
from jax.sharding import PartitionSpec as P

D = 4608
FFW = 18432
SEQ = 128
NSEG = 8
CORES = 2

EPSILON = 1e-06
CLIP_FRACTION = 4.2
MESH = pl.DeviceIdType.MESH


def clip_bound():
    return CLIP_FRACTION * (FFW * D * NSEG / SEQ) ** 0.5


def rows_of(index, count):
    return pl.ds(pl.multiple_of(index * count, count), count)


def kernel(
    ndp, nt, width, share, ids_in, hid_ref, grad_ref, noise_ref, out_ref, norms_ref,
    ids_ref, hall, g, gt, gt_in, wt, sq_t, sq_d,
    load_sem, hid_load, own_send, fwd_send, mate_send, hid_recv, gt_send, gt_recv,
    share_send, share_recv, sqt_send, sqt_recv, sqd_send, sqd_recv, chain,
):
    d = lax.axis_index("dp")
    t = lax.axis_index("tensor")
    nz = ndp // CORES
    z = lax.div(d, CORES)
    c = lax.rem(d, CORES)
    mate = d + 1 - 2 * c
    rows, cols = out_ref.shape
    nk = cols // width
    part = rows // share

    def remote(src, dst, send, recv, device):
        return pltpu.make_async_remote_copy(
            src_ref=src, dst_ref=dst, send_sem=send, recv_sem=recv, device_id=device, device_id_type=MESH
        )

    def others(count, me, body):
        def step(i, carry):
            body(lax.rem(me + i, count))
            return carry

        lax.fori_loop(1, count, step, 0)

    def repeat(low, high, body):
        def step(i, carry):
            body(i)
            return carry

        lax.fori_loop(low, high, step, 0)

    def load_h(k):
        return pltpu.make_async_copy(
            hid_ref.at[:, rows_of(k, width)], hall.at[k, rows_of(d, SEQ), :], hid_load.at[k]
        )

    load_g = pltpu.make_async_copy(grad_ref, g, load_sem.at[0])
    load_n = pltpu.make_async_copy(noise_ref, out_ref, load_sem.at[1])
    load_i = pltpu.make_async_copy(ids_in, ids_ref, load_sem.at[2])

    def tell(sem, **device):
        pl.semaphore_signal(sem, inc=1, device_id=device, device_id_type=MESH)

    barrier = pltpu.get_barrier_semaphore()
    tell(barrier, dp=mate)

    @pl.when(z + 1 < nz)
    def _():
        tell(barrier, dp=d + CORES)

    @pl.when(z == 0)
    def _():
        others(nt, t, lambda m: tell(barrier, tensor=m))

    repeat(0, nk, lambda k: load_h(k).start())
    load_g.start()
    load_i.start()

    @pl.when(z == 0)
    def _():
        pl.semaphore_wait(barrier, nt)

    @pl.when(z > 0)
    def _():
        pl.semaphore_wait(barrier, 2)
        tell(chain.at[4], dp=d - CORES)

    def chunk(j, k):
        return hall.at[k, rows_of(j, SEQ), :]

    def to(j, k, send, device):
        return remote(chunk(j, k), chunk(j, k), send, hid_recv.at[j, k], {"dp": device})

    def send_first(k):
        @pl.when(z > 0)
        def _():
            remote(
                hid_ref.at[:, rows_of(k, width)], chunk(d, k), own_send.at[1], hid_recv.at[d, k], {"dp": d - CORES}
            ).start()

    def send_mate(k):
        load_h(k).wait()
        to(d, k, mate_send.at[z], mate).start()

    def send_down(k):
        @pl.when(z > 0)
        def _():
            to(d, k, own_send.at[1], d - CORES).start()

    def send_up(k):
        @pl.when(z + 1 < nz)
        def _():
            to(d, k, own_send.at[0], d + CORES).start()

    def send_both(k):
        send_mate(k)
        send_down(k)
        send_up(k)

    early = min(2, nk)
    repeat(0, early, send_first)
    repeat(0, early, send_mate)

    @pl.when(z + 1 < nz)
    def _():
        pl.semaphore_wait(chain.at[4], 1)

    repeat(0, early, send_up)
    repeat(early, nk, send_both)
    load_n.start()

    load_g.wait()

    def turn(i):
        gt[rows_of(i, SEQ), :] = g[:, rows_of(i, SEQ)].T

    repeat(0, D // SEQ, turn)
    piece = (t if share > 1 else 0) * part

    def gt_copy(j, src_seq):
        return remote(
            gt.at[pl.ds(pl.multiple_of(j * rows + piece, 16), part), :],
            gt_in.at[src_seq, pl.ds(pl.multiple_of(piece, 16), part), :],
            gt_send.at[j], gt_recv.at[src_seq], {"dp": j},
        )

    gt_in[d, pl.ds(pl.multiple_of(piece, 16), part), :] = gt[pl.ds(pl.multiple_of(d * rows + piece, 16), part), :]

    def members(j):
        ids = ids_ref[pl.ds(j, 1), :]
        inside = (lax.broadcasted_iota(jnp.int32, (NSEG, SEQ), 0) == ids).astype(jnp.float32)
        return ids, inside, jnp.sum(inside, axis=1, keepdims=True)

    load_i.wait()
    ids, inside, count = members(d)
    contract = (((1,), (1,)), ((), ()))

    def gram(k, held):
        own = hall[k, rows_of(d, SEQ), :]
        return held + lax.dot_general(own, own, contract, preferred_element_type=jnp.float32)

    gram_hidden = lax.fori_loop(0, nk, gram, jnp.zeros((SEQ, SEQ), jnp.float32))
    gram_raw = lax.dot_general(g[...], g[...], contract, preferred_element_type=jnp.float32)
    wide = jnp.broadcast_to(ids.astype(jnp.float32), (SEQ, SEQ))
    pairs = jnp.where(wide == wide.T, gram_hidden * gram_raw, 0.0)
    per_token = jnp.sum(pairs, axis=0, keepdims=True)
    partial = jnp.sum(inside * per_token, axis=1, keepdims=True)
    sq_t[t] = jnp.broadcast_to(partial, (NSEG, SEQ))

    def sqt_copy(m, src):
        return remote(sq_t.at[src], sq_t.at[src], sqt_send.at[m], sqt_recv.at[src], {"tensor": m})

    @pl.when(z + 1 < nz)
    def _():
        pl.semaphore_wait(chain.at[0], 1)

    @pl.when(z > 0)
    def _():
        tell(chain.at[0], dp=d - CORES)
        pl.semaphore_wait(chain.at[3], 1)

    @pl.when(z == 0)
    def _():
        others(nt, t, lambda m: tell(chain.at[1], tensor=m))
        pl.semaphore_wait(chain.at[1], nt - 1)
        tell(chain.at[2], dp=mate)
        pl.semaphore_wait(chain.at[2], 1)

    @pl.when(z + 1 < nz)
    def _():
        tell(chain.at[3], dp=d + CORES)

    others(nt, t, lambda m: sqt_copy(m, t).start())
    others(ndp, d, lambda j: gt_copy(j, d).start())
    others(nt, t, lambda m: sqt_copy(m, m).wait_recv())
    total = sq_t[0]
    for m in range(1, nt):
        total = total + sq_t[m]
    total = total / (count * count)
    sq_d[d] = total
    norms_ref[...] = jnp.sqrt(total + EPSILON)[:, 0]

    def sqd_copy(j, src):
        return remote(sq_d.at[src], sq_d.at[src], sqd_send.at[j], sqd_recv.at[src], {"dp": j})

    others(ndp, d, lambda j: sqd_copy(j, d).start())

    def forward(h, k):
        for way in (1, -1):
            far = z + way * h
            ahead = z - way

            @pl.when((far >= 0) & (far < nz))
            def _():
                j = far * CORES + c
                to(j, k, mate_send.at[far], mate).wait_recv()

                @pl.when((ahead >= 0) & (ahead < nz))
                def _():
                    to(j, k, fwd_send.at[far], ahead * CORES + c).start()

                to(j, k, mate_send.at[far], mate).start()

    repeat(0, nk, lambda k: forward(1, k))

    others(ndp, d, lambda j: gt_copy(j, j).wait_recv())

    def share_copy(m, src):
        block = gt_in.at[:, pl.ds(pl.multiple_of(src * part, 16), part), :]
        return remote(block, block, share_send.at[m], share_recv.at[src], {"tensor": m})

    if share > 1:
        others(nt, t, lambda m: share_copy(m, t).start())
    repeat(nk, nk * (nz - 2), lambda i: forward(1 + lax.div(i, nk), lax.rem(i, nk)))
    if share > 1:
        others(nt, t, lambda m: share_copy(m, m).wait_recv())
    others(ndp, d, lambda j: sqd_copy(j, j).wait_recv())

    def weigh(j):
        _, inside, count = members(j)
        norm = jnp.sqrt(sq_d[j] + EPSILON)
        factor = jnp.minimum(1.0, clip_bound() / norm)
        tok_count = jnp.sum(inside * count, axis=0, keepdims=True)
        tok_factor = jnp.sum(inside * factor, axis=0, keepdims=True)
        scaled = (gt_in[j].astype(jnp.float32) / tok_count).astype(jnp.bfloat16)
        wt[:, rows_of(j, SEQ)] = (scaled.astype(jnp.float32) * tok_factor).astype(jnp.bfloat16)

    def sent(far, sem):
        block = hall.at[:, rows_of(far * CORES + c, SEQ), :]
        remote(block, block, sem, hid_recv.at[0, 0], {"dp": mate}).wait_send()

    @pl.when(z + 1 < nz)
    def _():
        sent(z, own_send.at[0])

    @pl.when(z > 0)
    def _():
        sent(z, own_send.at[1])

    sent(z, mate_send.at[z])
    others(ndp, d, lambda j: gt_copy(j, d).wait_send())
    others(ndp, d, lambda j: sqd_copy(j, d).wait_send())
    others(nt, t, lambda m: sqt_copy(m, t).wait_send())
    if share > 1:
        others(nt, t, lambda m: share_copy(m, t).wait_send())
    repeat(0, ndp, weigh)
    load_n.wait()

    def multiply(k):
        repeat(0, nz, lambda far: to(far * CORES + 1 - c, k, mate_send.at[far], mate).wait_recv())
        at = rows_of(k, width)
        summed = jnp.dot(wt[...], hall[k], preferred_element_type=jnp.float32)
        out_ref[:, at] = (summed + out_ref[:, at].astype(jnp.float32)).astype(jnp.bfloat16)

    def last(k):
        @pl.when(k < nk)
        def _():
            forward(nz - 1, k)

        @pl.when(k > 0)
        def _():
            multiply(k - 1)

    repeat(0, nk + 1, last)

    def sent_on(far):
        @pl.when(far != z)
        def _():
            sent(far, mate_send.at[far])

        @pl.when((z > 0) & (z < nz - 1) & (far != z))
        def _():
            sent(far, fwd_send.at[far])

    repeat(0, nz, sent_on)


def place(pieces, held_ref, held_norms_ref, out_ref, norms_ref, sem):
    part = out_ref.shape[0] // pieces
    copies = [pltpu.make_async_copy(held_norms_ref, norms_ref, sem.at[pieces])]
    for i in range(pieces):
        at = pl.ds(i * part, part)
        copies.append(pltpu.make_async_copy(held_ref.at[at, :], out_ref.at[at, :], sem.at[i]))
    for copy in copies:
        copy.start()
    for copy in copies:
        copy.wait()


def per_device(ndp, nt, hidden, grad_out, seg_ids, seg_counts, added_noise):
    rows, cols = added_noise.shape
    width = next(w for w in (256, 384, 128) if cols % w == 0)
    share = nt if rows % (16 * nt) == 0 else 1
    nz = ndp // CORES
    nk = cols // width
    dma = pltpu.SemaphoreType.DMA
    hbm = pl.BlockSpec(memory_space=pltpu.HBM)
    vmem = pl.BlockSpec(memory_space=pltpu.VMEM)
    out, norms = pl.pallas_call(
        functools.partial(kernel, ndp, nt, width, share),
        out_shape=(
            jax.ShapeDtypeStruct((rows, cols), jnp.bfloat16),
            jax.ShapeDtypeStruct((NSEG,), jnp.float32),
        ),
        in_specs=[hbm] * 4,
        out_specs=(vmem, vmem),
        scratch_shapes=[
            pltpu.VMEM((ndp, SEQ), jnp.int32),
            pltpu.VMEM((nk, ndp * SEQ, width), jnp.bfloat16),
            pltpu.VMEM((SEQ, D), jnp.bfloat16),
            pltpu.VMEM((D, SEQ), jnp.bfloat16),
            pltpu.VMEM((ndp, rows, SEQ), jnp.bfloat16),
            pltpu.VMEM((rows, ndp * SEQ), jnp.bfloat16),
            pltpu.VMEM((nt, NSEG, SEQ), jnp.float32),
            pltpu.VMEM((ndp, NSEG, SEQ), jnp.float32),
            dma((3,)), dma((nk,)), dma((2,)), dma((nz,)), dma((nz,)), dma((ndp, nk)), dma((ndp,)), dma((ndp,)),
            dma((nt,)), dma((nt,)), dma((nt,)), dma((nt,)), dma((ndp,)), dma((ndp,)),
            pltpu.SemaphoreType.REGULAR((5,)),
        ],
        compiler_params=pltpu.CompilerParams(
            collective_id=0, has_side_effects=True, vmem_limit_bytes=32 * 1024 * 1024
        ),
        cost_estimate=pl.CostEstimate(
            flops=2 * ndp * SEQ * rows * cols, bytes_accessed=4 * rows * cols, transcendentals=0
        ),
    )(
        *(
            pltpu.with_memory_space_constraint(x, pltpu.HBM)
            for x in (seg_ids.reshape(ndp, SEQ), hidden, grad_out, added_noise)
        )
    )
    pieces = 8 if rows % 128 == 0 else 9
    return pl.pallas_call(
        functools.partial(place, pieces),
        out_shape=(
            jax.ShapeDtypeStruct((rows, cols), jnp.bfloat16),
            jax.ShapeDtypeStruct((NSEG,), jnp.float32),
        ),
        in_specs=[pl.BlockSpec(memory_space=pl.ANY)] * 2,
        out_specs=(pl.BlockSpec(memory_space=pl.ANY),) * 2,
        scratch_shapes=[dma((pieces + 1,))],
        compiler_params=pltpu.CompilerParams(vmem_limit_bytes=1024 * 1024),
        cost_estimate=pl.CostEstimate(flops=0, bytes_accessed=4 * rows * cols, transcendentals=0),
    )(out, norms)


def solution(mesh):
    placed = (P("dp", "tensor"), P("dp", None), P(), P("dp"), P("dp", "tensor"))
    return jax.shard_map(
        functools.partial(per_device, mesh.shape["dp"], mesh.shape["tensor"]),
        mesh=mesh,
        in_specs=placed,
        out_specs=(P("dp", "tensor"), P("dp")),
        check_vma=False,
    )
```

```python
import functools
import math

import jax
import jax.numpy as jnp
from jax import lax
from jax.experimental import pallas as pl
from jax.experimental.pallas import tpu as pltpu
from jax.sharding import PartitionSpec as P

D = 4608
FFW = 18432
SEQ = 128
NSEG = 8
CORES = 2

EPSILON = 1e-06
CLIP_FRACTION = 4.2
MESH = pl.DeviceIdType.MESH


def clip_bound():
    return CLIP_FRACTION * (FFW * D * NSEG / SEQ) ** 0.5


def rows_of(index, count):
    return pl.ds(pl.multiple_of(index * count, count), count)


def kernel(
    ndp, nt, width, share, ids_in, hid_ref, grad_ref, noise_ref, out_ref, norms_ref,
    ids_ref, hall, g, gt, gt_in, wt, sq_t, sq_d,
    load_sem, hid_load, own_send, fwd_send, mate_send, hid_recv, gt_send, gt_recv,
    share_send, share_recv, sqt_send, sqt_recv, sqd_send, sqd_recv, chain,
):
    d = lax.axis_index("dp")
    t = lax.axis_index("tensor")
    nz = ndp // CORES
    z = lax.div(d, CORES)
    c = lax.rem(d, CORES)
    mate = d + 1 - 2 * c
    rows, cols = out_ref.shape
    nk = cols // width
    part = rows // share

    def remote(src, dst, send, recv, device):
        return pltpu.make_async_remote_copy(
            src_ref=src, dst_ref=dst, send_sem=send, recv_sem=recv, device_id=device, device_id_type=MESH
        )

    def others(count, me, body):
        def step(i, carry):
            body(lax.rem(me + i, count))
            return carry

        lax.fori_loop(1, count, step, 0)

    def repeat(low, high, body):
        def step(i, carry):
            body(i)
            return carry

        lax.fori_loop(low, high, step, 0)

    def load_h(k):
        return pltpu.make_async_copy(
            hid_ref.at[:, rows_of(k, width)], hall.at[k, rows_of(d, SEQ), :], hid_load.at[k]
        )

    load_g = pltpu.make_async_copy(grad_ref, g, load_sem.at[0])
    load_n = pltpu.make_async_copy(noise_ref, out_ref, load_sem.at[1])
    load_i = pltpu.make_async_copy(ids_in, ids_ref, load_sem.at[2])

    def tell(sem, **device):
        pl.semaphore_signal(sem, inc=1, device_id=device, device_id_type=MESH)

    barrier = pltpu.get_barrier_semaphore()
    tell(barrier, dp=mate)

    @pl.when(z + 1 < nz)
    def _():
        tell(barrier, dp=d + CORES)

    @pl.when(z == 0)
    def _():
        others(nt, t, lambda m: tell(barrier, tensor=m))

    repeat(0, nk, lambda k: load_h(k).start())
    load_g.start()
    load_i.start()

    @pl.when(z == 0)
    def _():
        pl.semaphore_wait(barrier, nt)

    @pl.when(z > 0)
    def _():
        pl.semaphore_wait(barrier, 2)
        tell(chain.at[4], dp=d - CORES)

    def chunk(j, k):
        return hall.at[k, rows_of(j, SEQ), :]

    def to(j, k, send, device):
        return remote(chunk(j, k), chunk(j, k), send, hid_recv.at[j, k], {"dp": device})

    def send_first(k):
        @pl.when(z > 0)
        def _():
            remote(
                hid_ref.at[:, rows_of(k, width)], chunk(d, k), own_send.at[1], hid_recv.at[d, k], {"dp": d - CORES}
            ).start()

    def send_mate(k):
        load_h(k).wait()
        to(d, k, mate_send.at[z], mate).start()

    def send_down(k):
        @pl.when(z > 0)
        def _():
            to(d, k, own_send.at[1], d - CORES).start()

    def send_up(k):
        @pl.when(z + 1 < nz)
        def _():
            to(d, k, own_send.at[0], d + CORES).start()

    def send_both(k):
        send_mate(k)
        send_down(k)
        send_up(k)

    early = min(2, nk)
    repeat(0, early, send_first)
    repeat(0, early, send_mate)

    @pl.when(z + 1 < nz)
    def _():
        pl.semaphore_wait(chain.at[4], 1)

    repeat(0, early, send_up)
    repeat(early, nk, send_both)
    load_n.start()

    load_g.wait()

    def turn(i):
        gt[rows_of(i, SEQ), :] = g[:, rows_of(i, SEQ)].T

    repeat(0, D // SEQ, turn)
    piece = (t if share > 1 else 0) * part

    def gt_copy(j, src_seq):
        return remote(
            gt.at[pl.ds(pl.multiple_of(j * rows + piece, 16), part), :],
            gt_in.at[src_seq, pl.ds(pl.multiple_of(piece, 16), part), :],
            gt_send.at[j], gt_recv.at[src_seq], {"dp": j},
        )

    gt_in[d, pl.ds(pl.multiple_of(piece, 16), part), :] = gt[pl.ds(pl.multiple_of(d * rows + piece, 16), part), :]

    def members(j):
        ids = ids_ref[pl.ds(j, 1), :]
        inside = (lax.broadcasted_iota(jnp.int32, (NSEG, SEQ), 0) == ids).astype(jnp.float32)
        return ids, inside, jnp.sum(inside, axis=1, keepdims=True)

    load_i.wait()
    ids, inside, count = members(d)
    contract = (((1,), (1,)), ((), ()))

    def gram(k, held):
        own = hall[k, rows_of(d, SEQ), :]
        return held + lax.dot_general(own, own, contract, preferred_element_type=jnp.float32)

    gram_hidden = lax.fori_loop(0, nk, gram, jnp.zeros((SEQ, SEQ), jnp.float32))
    gram_raw = lax.dot_general(g[...], g[...], contract, preferred_element_type=jnp.float32)
    wide = jnp.broadcast_to(ids.astype(jnp.float32), (SEQ, SEQ))
    pairs = jnp.where(wide == wide.T, gram_hidden * gram_raw, 0.0)
    per_token = jnp.sum(pairs, axis=0, keepdims=True)
    partial = jnp.sum(inside * per_token, axis=1, keepdims=True)
    sq_t[t] = jnp.broadcast_to(partial, (NSEG, SEQ))

    def sqt_copy(m, src):
        return remote(sq_t.at[src], sq_t.at[src], sqt_send.at[m], sqt_recv.at[src], {"tensor": m})

    @pl.when(z + 1 < nz)
    def _():
        pl.semaphore_wait(chain.at[0], 1)

    @pl.when(z > 0)
    def _():
        tell(chain.at[0], dp=d - CORES)
        pl.semaphore_wait(chain.at[3], 1)

    @pl.when(z == 0)
    def _():
        others(nt, t, lambda m: tell(chain.at[1], tensor=m))
        pl.semaphore_wait(chain.at[1], nt - 1)
        tell(chain.at[2], dp=mate)
        pl.semaphore_wait(chain.at[2], 1)

    @pl.when(z + 1 < nz)
    def _():
        tell(chain.at[3], dp=d + CORES)

    others(nt, t, lambda m: sqt_copy(m, t).start())
    others(ndp, d, lambda j: gt_copy(j, d).start())
    others(nt, t, lambda m: sqt_copy(m, m).wait_recv())
    total = sq_t[0]
    for m in range(1, nt):
        total = total + sq_t[m]
    total = total / (count * count)
    sq_d[d] = total
    norms_ref[...] = jnp.sqrt(total + EPSILON)[:, 0]

    def sqd_copy(j, src):
        return remote(sq_d.at[src], sq_d.at[src], sqd_send.at[j], sqd_recv.at[src], {"dp": j})

    others(ndp, d, lambda j: sqd_copy(j, d).start())

    def forward(h, k):
        for way in (1, -1):
            far = z + way * h
            ahead = z - way

            @pl.when((far >= 0) & (far < nz))
            def _():
                j = far * CORES + c
                to(j, k, mate_send.at[far], mate).wait_recv()

                @pl.when((ahead >= 0) & (ahead < nz))
                def _():
                    to(j, k, fwd_send.at[far], ahead * CORES + c).start()

                to(j, k, mate_send.at[far], mate).start()

    repeat(0, nk, lambda k: forward(1, k))

    others(ndp, d, lambda j: gt_copy(j, j).wait_recv())

    def share_copy(m, src):
        block = gt_in.at[:, pl.ds(pl.multiple_of(src * part, 16), part), :]
        return remote(block, block, share_send.at[m], share_recv.at[src], {"tensor": m})

    if share > 1:
        others(nt, t, lambda m: share_copy(m, t).start())
    repeat(nk, nk * (nz - 2), lambda i: forward(1 + lax.div(i, nk), lax.rem(i, nk)))
    if share > 1:
        others(nt, t, lambda m: share_copy(m, m).wait_recv())
    others(ndp, d, lambda j: sqd_copy(j, j).wait_recv())

    def weigh(j):
        _, inside, count = members(j)
        norm = jnp.sqrt(sq_d[j] + EPSILON)
        factor = jnp.minimum(1.0, clip_bound() / norm)
        tok_count = jnp.sum(inside * count, axis=0, keepdims=True)
        tok_factor = jnp.sum(inside * factor, axis=0, keepdims=True)
        scaled = (gt_in[j].astype(jnp.float32) / tok_count).astype(jnp.bfloat16)
        wt[:, rows_of(j, SEQ)] = (scaled.astype(jnp.float32) * tok_factor).astype(jnp.bfloat16)

    def sent(far, sem):
        block = hall.at[:, rows_of(far * CORES + c, SEQ), :]
        remote(block, block, sem, hid_recv.at[0, 0], {"dp": mate}).wait_send()

    @pl.when(z + 1 < nz)
    def _():
        sent(z, own_send.at[0])

    @pl.when(z > 0)
    def _():
        sent(z, own_send.at[1])

    sent(z, mate_send.at[z])
    others(ndp, d, lambda j: gt_copy(j, d).wait_send())
    others(ndp, d, lambda j: sqd_copy(j, d).wait_send())
    others(nt, t, lambda m: sqt_copy(m, t).wait_send())
    if share > 1:
        others(nt, t, lambda m: share_copy(m, t).wait_send())
    repeat(0, ndp, weigh)
    load_n.wait()

    def multiply(k):
        repeat(0, nz, lambda far: to(far * CORES + 1 - c, k, mate_send.at[far], mate).wait_recv())
        at = rows_of(k, width)
        summed = jnp.dot(wt[...], hall[k], preferred_element_type=jnp.float32)
        out_ref[:, at] = (summed + out_ref[:, at].astype(jnp.float32)).astype(jnp.bfloat16)

    def last(k):
        @pl.when(k < nk)
        def _():
            forward(nz - 1, k)

        @pl.when(k > 0)
        def _():
            multiply(k - 1)

    repeat(0, nk + 1, last)

    def sent_on(far):
        @pl.when(far != z)
        def _():
            sent(far, mate_send.at[far])

        @pl.when((z > 0) & (z < nz - 1) & (far != z))
        def _():
            sent(far, fwd_send.at[far])

    repeat(0, nz, sent_on)


def place(pieces, held_ref, held_norms_ref, out_ref, norms_ref, sem):
    part = out_ref.shape[0] // pieces
    copies = [pltpu.make_async_copy(held_norms_ref, norms_ref, sem.at[pieces])]
    for i in range(pieces):
        at = pl.ds(i * part, part)
        copies.append(pltpu.make_async_copy(held_ref.at[at, :], out_ref.at[at, :], sem.at[i]))
    for copy in copies:
        copy.start()
    for copy in copies:
        copy.wait()


def per_device(ndp, nt, hidden, grad_out, seg_ids, seg_counts, added_noise):
    rows, cols = added_noise.shape
    width = next(w for w in (384, 256, 128) if cols % w == 0)
    share = nt if rows % (16 * nt) == 0 else 1
    nz = ndp // CORES
    nk = cols // width
    dma = pltpu.SemaphoreType.DMA
    hbm = pl.BlockSpec(memory_space=pltpu.HBM)
    vmem = pl.BlockSpec(memory_space=pltpu.VMEM)
    out, norms = pl.pallas_call(
        functools.partial(kernel, ndp, nt, width, share),
        out_shape=(
            jax.ShapeDtypeStruct((rows, cols), jnp.bfloat16),
            jax.ShapeDtypeStruct((NSEG,), jnp.float32),
        ),
        in_specs=[hbm] * 4,
        out_specs=(vmem, vmem),
        scratch_shapes=[
            pltpu.VMEM((ndp, SEQ), jnp.int32),
            pltpu.VMEM((nk, ndp * SEQ, width), jnp.bfloat16),
            pltpu.VMEM((SEQ, D), jnp.bfloat16),
            pltpu.VMEM((D, SEQ), jnp.bfloat16),
            pltpu.VMEM((ndp, rows, SEQ), jnp.bfloat16),
            pltpu.VMEM((rows, ndp * SEQ), jnp.bfloat16),
            pltpu.VMEM((nt, NSEG, SEQ), jnp.float32),
            pltpu.VMEM((ndp, NSEG, SEQ), jnp.float32),
            dma((3,)), dma((nk,)), dma((2,)), dma((nz,)), dma((nz,)), dma((ndp, nk)), dma((ndp,)), dma((ndp,)),
            dma((nt,)), dma((nt,)), dma((nt,)), dma((nt,)), dma((ndp,)), dma((ndp,)),
            pltpu.SemaphoreType.REGULAR((5,)),
        ],
        compiler_params=pltpu.CompilerParams(
            collective_id=0, has_side_effects=True, vmem_limit_bytes=32 * 1024 * 1024
        ),
        cost_estimate=pl.CostEstimate(
            flops=2 * ndp * SEQ * rows * cols, bytes_accessed=4 * rows * cols, transcendentals=0
        ),
    )(
        *(
            pltpu.with_memory_space_constraint(x, pltpu.HBM)
            for x in (seg_ids.reshape(ndp, SEQ), hidden, grad_out, added_noise)
        )
    )
    pieces = 8 if rows % 128 == 0 else 9
    return pl.pallas_call(
        functools.partial(place, pieces),
        out_shape=(
            jax.ShapeDtypeStruct((rows, cols), jnp.bfloat16),
            jax.ShapeDtypeStruct((NSEG,), jnp.float32),
        ),
        in_specs=[pl.BlockSpec(memory_space=pl.ANY)] * 2,
        out_specs=(pl.BlockSpec(memory_space=pl.ANY),) * 2,
        scratch_shapes=[dma((pieces + 1,))],
        compiler_params=pltpu.CompilerParams(vmem_limit_bytes=1024 * 1024),
        cost_estimate=pl.CostEstimate(flops=0, bytes_accessed=4 * rows * cols, transcendentals=0),
    )(out, norms)


def solution(mesh):
    placed = (P("dp", "tensor"), P("dp", None), P(), P("dp"), P("dp", "tensor"))
    return jax.shard_map(
        functools.partial(per_device, mesh.shape["dp"], mesh.shape["tensor"]),
        mesh=mesh,
        in_specs=placed,
        out_specs=(P("dp", "tensor"), P("dp")),
        check_vma=False,
    )
```
